512 devices in a mesh: dp: 128 (over z, y, core), mp: 4 (over x).
Axes of the slice: x: 4, y: 8, z: 8, core: 2. Of those that a mesh axis runs over, the one named last changes fastest.
Arguments:
- query_states: bfloat16 [16384, 4096], P('dp', 'mp'), may hold values from -6 to 6
- passage_states: bfloat16 [16384, 4096], P('dp', 'mp'), may hold values from -6 to 6
- head_weight: bfloat16 [4096, 4096], P('dp', 'mp'), may hold values from -0.09375 to 0.09375
- positives: int32 [16384], P('dp'), may hold values from 0 to 127
- negatives: int32 [16384, 1], P('dp'), may hold values from 0 to 127; in each aligned block of 128 rows (0 to 127, 128 to 255, ...) at most 2 rows name the same one
Outputs:
- query_grads: float32 [16384, 4096], P('dp', 'mp')
- passage_grads: float32 [16384, 4096], P('dp', 'mp')
The draws below stay inside these ranges and needn't reach their ends.
Inputs may be any that keep to these rules, and one draw needn't show every extreme that they name: `positives`: positives_i indexes the 128 passages of query i's own shard, in that shard's order. `negatives`: the 1 block of a query are different; block b lies on shard b. Among the 128 queries of one shard no block is named more than 2 times, and in some shards some block is named exactly 2 times.
All inputs are finite; a program needn't handle non-finite values.
Results may differ from the reference program's by a relative error of at most 0.0038.
Values may be sent and summed in bfloat16 or wider, within the bound.
No kernel may reach another device: no remote copies, remote signals or barrier semaphores. Data moves between devices by JAX's collectives and lax.ppermute only.
A program may use at most 128 MiB of HBM per device.

```python
import math
import jax
import jax.numpy as jnp
import numpy as np
from jax import lax

D = 4096
E = 4096
PAIRS = 128
BLOCK = 128
HARD = 1
BLOCKS = 128
CAPACITY = 2
QUERIES = 16384
N_DP = 128


def touch_ends(values, own_key, low, top_value):
    place = [jax.random.randint(jax.random.fold_in(own_key, axis), (), 0, length) for axis, length in enumerate(values.shape)]
    widest = values.shape.index(max(values.shape))
    neighbour = place[:widest] + [(place[widest] + 1) % values.shape[widest]] + place[widest + 1:]
    return values.at[tuple(place)].set(low).at[tuple(neighbour)].set(top_value)


def steps_of(stream_key, extent, split, low, top_value):
    def one(position, parts):
        steps = jax.random.uniform(jax.random.fold_in(jax.random.fold_in(stream_key, 6), position), (parts,), jnp.float32, low / len(split), top_value / len(split))
        return jnp.repeat(jnp.exp(steps), extent[position] // parts).reshape((-1,) + (1,) * (len(extent) - position - 1))

    gain = one(*split[0])
    for cut in split[1:]:
        gain = gain * one(*cut)
    return gain


def routed_block(stream_key, own, number, rows, number_of, top, bound, skew):
    order = jax.random.permutation(stream_key, number_of)
    heavy_load, usual = portions_of(number_of, rows * top, bound, skew, True), portions_of(number_of, rows * top, bound, skew, False)
    places = jnp.arange(number_of)

    def named(sizes, rotation):
        used = int((sizes > 0).sum())
        fixed = max(1, used // 4)
        passed = fixed + (places - fixed + rotation * (used - fixed)) % max(1, number_of - fixed)
        return jnp.zeros((number_of,), jnp.int32).at[order[jnp.where(places < fixed, places, passed)]].set(jnp.asarray(sizes, jnp.int32))

    sizes = jnp.where(number % 4 == 0, named(heavy_load, number // 4), named(usual, number - number // 4 - 1))
    mixed = jax.random.permutation(jax.random.fold_in(own, 3), number_of)
    source_of, receiver = mixed[0:number_of // 2 * 2:2], mixed[1:number_of // 2 * 2:2]
    margin = jnp.minimum(sizes[source_of] - 1, bound - sizes[receiver]) // 2
    margin = jnp.where((source_of == order[0]) | (receiver == order[0]) | (sizes[receiver] == 0), 0, jnp.maximum(margin, 0))
    passed = jax.random.randint(jax.random.fold_in(own, 4), (number_of // 2,), 0, 1 << 20) % (margin + 1)
    sizes = sizes.at[source_of].add(-passed).at[receiver].add(passed)
    members = jnp.searchsorted(jnp.cumsum(sizes), jnp.arange(rows * top), side="right").astype(jnp.int32)
    listing = members.reshape(top, rows).T
    listing = listing[jax.random.permutation(jax.random.fold_in(own, 1), rows)]
    rotation = jax.random.randint(jax.random.fold_in(own, 2), (rows, 1), 0, top)
    return jnp.take_along_axis(listing, (jnp.arange(top)[None, :] + rotation) % top, axis=1)


def portions_of(number_of, total, bound, skew, full):
    weights = [(1 << 20) // math.isqrt(rank ** skew) + 1 for rank in range(1, number_of + 1)]
    largest = bound if full else min(bound, max(-(-total // number_of), total * weights[0] // sum(weights)))
    least = 1 if total - largest >= number_of - 1 else 0
    counts, spare = [largest] + [least] * (number_of - 1), total - largest - least * (number_of - 1)
    while spare > 0:
        free = [i for i in range(1, number_of) if counts[i] < largest] or [i for i in range(1, number_of) if counts[i] < bound]
        pool, left = sum([weights[i] for i in free]), spare
        for i in free:
            addition = min(bound - counts[i], max(1, left * weights[i] // pool), spare)
            counts[i] = counts[i] + addition
            spare = spare - addition
    return np.array(counts)


def normal_values(rng, shape, deviation, reach, split=(), held_as=jnp.bfloat16):
    gain = steps_of(rng, shape, split, -0.22, 0.18) if split else 1.0
    result = jax.random.normal(rng, shape, jnp.float32) * deviation * gain
    return jnp.minimum(jnp.maximum(result, -reach), reach).astype(held_as)


def setup_inputs(seed: int = 0) -> dict:
    key_list = jax.random.split(jax.random.key(seed), 6)
    query_states = normal_values(key_list[0], (QUERIES, D), 1.0, 6.0, ((0, 128), (1, 4)))
    passage_states = normal_values(key_list[1], (QUERIES, D), 1.0, 6.0, ((0, 128), (1, 4)))
    head_weight = normal_values(key_list[2], (E, D), D ** -0.5, 0.09375, ((0, 128), (1, 4)))
    positives = touch_ends(jax.random.randint(key_list[3], (QUERIES,), 0, PAIRS), jax.random.fold_in(key_list[3], 1), 0, PAIRS - 1).astype(jnp.int32)
    negatives_keys = jax.random.split(jax.random.fold_in(key_list[4], 1), QUERIES // PAIRS)
    negatives_turns = jax.random.permutation(jax.random.fold_in(key_list[4], 3), QUERIES // PAIRS)
    negatives = jax.vmap(lambda own, number: routed_block(jax.random.fold_in(key_list[4], 2), own, number, PAIRS, BLOCKS, HARD, CAPACITY, 2))(negatives_keys, negatives_turns).reshape((QUERIES, HARD))
    return dict(query_states=query_states, passage_states=passage_states, head_weight=head_weight, positives=positives, negatives=negatives)


SCORE_SCALE = 80.0
GRADIENT_SCALE = 2560.0
EPSILON = 1e-06

def project_rows(states, head_weight):
    projected = jnp.dot(states, head_weight.T, preferred_element_type=jnp.float32)
    inverse = lax.rsqrt(lax.optimization_barrier(jnp.sum(projected * projected, axis=1, keepdims=True)) + EPSILON)
    return (projected, inverse, (projected * inverse).astype(jnp.bfloat16))

def row_backward(projected, inverse, grad_embedded, head_weight):
    radial = lax.optimization_barrier(jnp.sum(projected * grad_embedded, axis=1, keepdims=True))
    proj_grad = (inverse * grad_embedded - projected * (inverse * inverse * inverse) * radial).astype(jnp.bfloat16)
    return jnp.dot(proj_grad, head_weight, preferred_element_type=jnp.float32)

def reference(query_states, passage_states, head_weight, positives, negatives):
    query_proj, query_inverse, query_embedded = project_rows(query_states, head_weight)
    passage_proj, passage_inverse, passage_embedded = project_rows(passage_states, head_weight)
    passage_blocks = passage_embedded.reshape(BLOCKS, BLOCK, E)
    pair_query = jnp.repeat(jnp.arange(QUERIES, dtype=jnp.int32), HARD)
    pair_block = negatives.reshape(-1).astype(jnp.int32)

    def hard_forward(element):
        query_row, block_id = element
        query_vector = lax.dynamic_index_in_dim(query_embedded, query_row, 0, keepdims=False)
        block_rows = lax.dynamic_index_in_dim(passage_blocks, block_id, 0, keepdims=False)
        pair_exp = jnp.exp(SCORE_SCALE * jnp.dot(block_rows, query_vector, preferred_element_type=jnp.float32))
        weighted = jnp.dot(pair_exp.astype(jnp.bfloat16), block_rows, preferred_element_type=jnp.float32)
        return (pair_exp, weighted)
    hard_exp, hard_parts = lax.map(hard_forward, (pair_query, pair_block))
    hard_totals = lax.optimization_barrier(jnp.sum(hard_exp, axis=1)).reshape(N_DP, PAIRS, HARD).sum(axis=2)
    hard_sums = hard_parts.reshape(N_DP, PAIRS, HARD, E).sum(axis=2)

    def local_shard(element):
        queries, passages, positive_rows, extra_totals, extra_sums = element
        local_exp = jnp.exp(SCORE_SCALE * jnp.dot(queries, passages.T, preferred_element_type=jnp.float32))
        totals = lax.optimization_barrier(jnp.sum(local_exp, axis=1)) + extra_totals
        positive_mask = (positive_rows[:, None] == jnp.arange(PAIRS, dtype=jnp.int32)[None, :]).astype(jnp.float32)
        local_coef = (GRADIENT_SCALE * (local_exp / totals[:, None] - positive_mask)).astype(jnp.bfloat16)
        query_grad = jnp.dot(local_coef, passages, preferred_element_type=jnp.float32) + (GRADIENT_SCALE / totals)[:, None] * extra_sums
        passage_grad = jnp.dot(local_coef.T, queries, preferred_element_type=jnp.float32)
        return (totals, query_grad, passage_grad)
    totals, query_grad, passage_grad = lax.map(local_shard, (query_embedded.reshape(N_DP, PAIRS, E), passage_embedded.reshape(N_DP, PAIRS, E), positives.reshape(N_DP, PAIRS).astype(jnp.int32), hard_totals, hard_sums))
    totals = totals.reshape(QUERIES)

    def hard_backward(accumulated, element):
        query_row, block_id, pair_exp = element
        query_vector = lax.dynamic_index_in_dim(query_embedded, query_row, 0, keepdims=False).astype(jnp.float32)
        query_total = lax.dynamic_index_in_dim(totals, query_row, 0, keepdims=False)
        rounded = lax.optimization_barrier((GRADIENT_SCALE * pair_exp / query_total).astype(jnp.bfloat16))
        hard_coef = rounded.astype(jnp.float32)
        block_grad = lax.dynamic_index_in_dim(accumulated, block_id, 0, keepdims=False) + hard_coef[:, None] * query_vector[None, :]
        return (lax.dynamic_update_index_in_dim(accumulated, block_grad, block_id, 0), None)
    remote_grad = lax.scan(hard_backward, jnp.zeros((BLOCKS, BLOCK, E), jnp.float32), (pair_query, pair_block, hard_exp))[0]
    passage_total = passage_grad.reshape(QUERIES, E) + remote_grad.reshape(QUERIES, E)
    query_out = row_backward(query_proj, query_inverse, query_grad.reshape(QUERIES, E), head_weight)
    passage_out = row_backward(passage_proj, passage_inverse, passage_total, head_weight)
    return (query_out, passage_out)
```

```python
import jax
import jax.numpy as jnp
from jax import lax
from jax.sharding import PartitionSpec as P

CAPACITY = 2
SCORE_SCALE = 80.0
GRADIENT_SCALE = 2560.0
EPSILON = 1e-06
LAST_BOTH = (((1,), (1,)), ((), ()))
FIRST_BOTH = (((0,), (0,)), ((), ()))
F32 = jnp.float32
BF16 = jnp.bfloat16


def dot(a, b, dims=(((1,), (0,)), ((), ()))):
    return lax.dot_general(a, b, dims, preferred_element_type=F32)


def swap(x, axis):
    return lax.all_to_all(x, axis, split_axis=0, concat_axis=0, tiled=True)


def from_all(x, axis):
    return swap(jnp.broadcast_to(x[None], (lax.axis_size(axis),) + x.shape), axis)


def sum_all(x, axis):
    return jnp.sum(from_all(x, axis), axis=0)


def on_device(query_states, passage_states, head_weight, positives, negatives):
    pairs, width = query_states.shape
    parts = lax.axis_size("mp")
    shards = lax.axis_size("dp")
    own_rows = head_weight.shape[0] // parts
    slots = shards * CAPACITY

    weight_rows = swap(head_weight.reshape(parts, own_rows, width), "mp")
    weight_rows = weight_rows.transpose(1, 0, 2).reshape(own_rows, parts * width)
    weight = lax.all_gather(weight_rows, "dp", axis=0, tiled=True)
    states = jnp.concatenate([query_states, passage_states], axis=0)
    states = from_all(states, "mp").transpose(1, 0, 2).reshape(2 * pairs, parts * width)

    block = negatives.reshape(-1)
    order = jnp.arange(pairs, dtype=jnp.int32)
    earlier = (block[:, None] == block[None, :]) & (order[None, :] < order[:, None])
    slot = block * CAPACITY + jnp.sum(earlier.astype(jnp.int32), axis=1)
    in_slot = jnp.arange(slots, dtype=jnp.int32)[:, None] == slot[None, :]
    to_slot = in_slot.astype(BF16)
    positive_mask = (positives[:, None] == order[None, :]).astype(F32)

    projected = dot(states, weight, LAST_BOTH)
    squares = lax.psum(jnp.sum(projected * projected, axis=1), "mp")
    inverse = lax.rsqrt(squares[:, None] + EPSILON)
    embedded = (projected * inverse).astype(BF16)
    query, passage = embedded[:pairs], embedded[pairs:]
    part = query.shape[1]

    outgoing = dot(to_slot, query).astype(BF16)
    arrived = swap(outgoing.reshape(shards, CAPACITY, part), "dp").reshape(slots, part)

    local_scores = sum_all(dot(query, passage, LAST_BOTH), "mp")
    local_exp = jnp.exp(SCORE_SCALE * local_scores)
    local_totals = jnp.sum(local_exp, axis=1)
    slot_totals = jnp.sum(jnp.where(in_slot, local_totals[None, :], 0.0), axis=1)
    slot_totals = swap(slot_totals.reshape(shards, 1, CAPACITY), "dp").reshape(slots)

    hard_scores = sum_all(dot(arrived, passage, LAST_BOTH), "mp")
    hard_exp = jnp.exp(SCORE_SCALE * hard_scores)
    hard_totals = jnp.sum(hard_exp, axis=1)
    scale = GRADIENT_SCALE / (slot_totals + hard_totals)
    rounded_exp = hard_exp.astype(BF16)
    hard_radial = scale * jnp.sum(rounded_exp.astype(F32) * hard_scores, axis=1)
    back = jnp.stack([hard_totals, hard_radial], axis=1).reshape(shards, 1, 2 * CAPACITY)
    back = swap(back, "dp").reshape(slots, 2)
    hard_sums = (scale[:, None] * dot(rounded_exp, passage)).astype(BF16)
    hard_sums = swap(hard_sums.reshape(shards, CAPACITY, part), "dp").reshape(slots, part)
    hard_coef = (hard_exp * scale[:, None]).astype(BF16)

    back = jnp.sum(jnp.where(in_slot[:, :, None], back[:, None, :], 0.0), axis=0)
    totals = local_totals + back[:, 0]
    local_coef = (
        GRADIENT_SCALE * (local_exp / totals[:, None] - positive_mask)
    ).astype(BF16)
    weighted_scores = local_coef.astype(F32) * local_scores

    def state_grad(rows, grad, radial):
        inv = inverse[rows]
        proj_grad = (inv * grad - projected[rows] * (inv * inv * radial[:, None])).astype(BF16)
        partial = dot(proj_grad, weight).astype(BF16)
        partial = partial.reshape(pairs, parts, width).transpose(1, 0, 2)
        return jnp.sum(swap(partial, "mp").astype(F32), axis=0)

    passage_grad = dot(local_coef, query, FIRST_BOTH) + dot(hard_coef, arrived, FIRST_BOTH)
    passage_radial = jnp.sum(weighted_scores, axis=0) + jnp.sum(
        hard_coef.astype(F32) * hard_scores, axis=0
    )
    passage_out = state_grad(slice(pairs, None), passage_grad, passage_radial)

    query_grad = dot(local_coef, passage) + dot(to_slot, hard_sums, FIRST_BOTH)
    query_radial = jnp.sum(weighted_scores, axis=1) + back[:, 1]
    query_out = state_grad(slice(0, pairs), query_grad, query_radial)
    return (query_out, passage_out)


def solution(mesh):
    in_specs = (P("dp", "mp"), P("dp", "mp"), P("dp", "mp"), P("dp"), P("dp", None))
    out_specs = (P("dp", "mp"), P("dp", "mp"))
    return jax.shard_map(
        on_device, mesh=mesh, in_specs=in_specs, out_specs=out_specs, check_vma=False
    )
```

```python
import math

import jax
import jax.numpy as jnp
from jax import lax
from jax.sharding import PartitionSpec as P

CAPACITY = 2
CORES = 2
EXTRA = 128
SCORE_SCALE = 80.0
GRADIENT_SCALE = 2560.0
EPSILON = 1e-06
LAST_BOTH = (((1,), (1,)), ((), ()))
FIRST_BOTH = (((0,), (0,)), ((), ()))
F32 = jnp.float32
BF16 = jnp.bfloat16


def dot(a, b, dims=(((1,), (0,)), ((), ()))):
    return lax.dot_general(a, b, dims, preferred_element_type=F32)


def swap(x, axis, groups=None):
    return lax.all_to_all(
        x, axis, split_axis=0, concat_axis=0, tiled=True, axis_index_groups=groups
    )


def from_all(x, axis):
    return swap(jnp.broadcast_to(x[None], (lax.axis_size(axis),) + x.shape), axis)


def sum_all(x, axis):
    return jnp.sum(from_all(x, axis), axis=0)


def parts_of(x, count):
    out = []
    for _ in range(count):
        part = lax.reduce_precision(x, 8, 7)
        out.append(part.astype(BF16))
        x = x - part
    return out


def columns(parts):
    stacked = jnp.stack(parts, axis=1)
    return jnp.pad(stacked, ((0, 0), (0, EXTRA - len(parts))))


def lines(shards, parts):
    side = math.isqrt(shards // CORES)

    def shard(z, y, core):
        return (z * side + y) * CORES + core

    first = [
        [shard(z, y, 0) * parts + m for m in range(parts) for y in range(side)]
        for z in range(side)
    ] + [
        [shard(z, y, 1) * parts + m for m in range(parts) for z in range(side)]
        for y in range(side)
    ]
    second = [[shard(z, y, 0) for z in range(side)] for y in range(side)] + [
        [shard(z, y, 1) for y in range(side)] for z in range(side)
    ]
    other_core = [(d, d ^ 1) for d in range(shards)]
    return side, first, second, other_core


def on_device(query_states, passage_states, head_weight, positives, negatives):
    pairs, width = query_states.shape
    parts = lax.axis_size("mp")
    shards = lax.axis_size("dp")
    slots = shards * CAPACITY
    side, first, second, other_core = lines(shards, parts)
    rows = head_weight.shape[0] // parts
    core = lax.axis_index("dp") % CORES

    line = jnp.broadcast_to(
        head_weight.reshape(parts, 1, rows, width), (parts, side, rows, width)
    ).reshape(parts * side, rows, width)
    line = swap(line, ("dp", "mp"), first).reshape(parts, side, rows, width)
    line = line.transpose(1, 2, 0, 3).reshape(side * rows, parts * width)
    weight_own = lax.all_gather(line, "dp", axis=0, tiled=True, axis_index_groups=second)
    weight_other = lax.ppermute(weight_own, "dp", other_core)
    states = jnp.concatenate([query_states, passage_states], axis=0)
    states = from_all(states, "mp").transpose(1, 0, 2).reshape(2 * pairs, parts * width)

    block = negatives.reshape(-1)
    order = jnp.arange(pairs, dtype=jnp.int32)
    earlier = (block[:, None] == block[None, :]) & (order[None, :] < order[:, None])
    slot = block * CAPACITY + jnp.sum(earlier.astype(jnp.int32), axis=1)
    in_slot = jnp.arange(slots, dtype=jnp.int32)[:, None] == slot[None, :]
    to_slot = in_slot.astype(BF16)
    positive_mask = (positives[:, None] == order[None, :]).astype(F32)

    def in_order(own, other):
        return jnp.where(core == 0, own, other), jnp.where(core == 0, other, own)

    projected_own = dot(states, weight_own, LAST_BOTH)
    projected_other = dot(states, weight_other, LAST_BOTH)
    squares = jnp.sum(projected_own * projected_own, axis=1) + jnp.sum(
        projected_other * projected_other, axis=1
    )
    projected = jnp.concatenate(in_order(projected_own, projected_other), axis=1)
    squares = sum_all(squares.reshape(-1, math.gcd(128, 2 * pairs)), "mp").reshape(-1)
    inverse = lax.rsqrt(squares[:, None] + EPSILON)
    embedded = (projected * inverse).astype(BF16)
    query, passage = embedded[:pairs], embedded[pairs:]
    part = query.shape[1]

    local_scores = sum_all(dot(query, passage, LAST_BOTH), "mp")
    local_exp = jnp.exp(SCORE_SCALE * local_scores)
    local_totals = jnp.sum(local_exp, axis=1)

    def exchange(message):
        message = message.reshape(shards, CAPACITY, part + EXTRA)
        return swap(message, "dp").reshape(slots, part + EXTRA)

    outgoing = jnp.concatenate([query, columns(parts_of(local_totals, 3))], axis=1)
    arrived = exchange(dot(to_slot, outgoing).astype(BF16))
    slot_totals = jnp.sum(arrived[:, part : part + 3].astype(F32), axis=1)
    arrived = arrived[:, :part]

    hard_scores = sum_all(dot(arrived, passage, LAST_BOTH), "mp")
    hard_exp = jnp.exp(SCORE_SCALE * hard_scores)
    hard_totals = jnp.sum(hard_exp, axis=1)
    scale = GRADIENT_SCALE / (slot_totals + hard_totals)
    rounded_exp = hard_exp.astype(BF16)
    hard_radial = scale * jnp.sum(rounded_exp.astype(F32) * hard_scores, axis=1)
    hard_sums = (scale[:, None] * dot(rounded_exp, passage)).astype(BF16)
    back = columns(parts_of(hard_totals, 3) + parts_of(hard_radial, 3))
    back = exchange(jnp.concatenate([hard_sums, back], axis=1))
    back = dot(to_slot, back, FIRST_BOTH)
    hard_coef = (hard_exp * scale[:, None]).astype(BF16)

    totals = local_totals + jnp.sum(back[:, part : part + 3], axis=1)
    local_coef = (
        GRADIENT_SCALE * (local_exp / totals[:, None] - positive_mask)
    ).astype(BF16)
    weighted_scores = local_coef.astype(F32) * local_scores

    query_grad = dot(local_coef, passage) + back[:, :part]
    query_radial = jnp.sum(weighted_scores, axis=1) + jnp.sum(
        back[:, part + 3 : part + 6], axis=1
    )
    passage_grad = dot(local_coef, query, FIRST_BOTH) + dot(hard_coef, arrived, FIRST_BOTH)
    passage_radial = jnp.sum(weighted_scores, axis=0) + jnp.sum(
        hard_coef.astype(F32) * hard_scores, axis=0
    )
    grad = jnp.concatenate([query_grad, passage_grad], axis=0)
    radial = jnp.concatenate([query_radial, passage_radial], axis=0)[:, None]
    proj_grad = (inverse * grad - projected * (inverse * inverse * radial)).astype(BF16)
    grad_own, grad_other = in_order(proj_grad[:, : part // 2], proj_grad[:, part // 2 :])
    partial = (dot(grad_own, weight_own) + dot(grad_other, weight_other)).astype(BF16)
    partial = partial.reshape(2 * pairs, parts, width).transpose(1, 0, 2)
    state_grad = jnp.sum(swap(partial, "mp").astype(F32), axis=0)
    return (state_grad[:pairs], state_grad[pairs:])


def solution(mesh):
    in_specs = (P("dp", "mp"), P("dp", "mp"), P("dp", "mp"), P("dp"), P("dp", None))
    out_specs = (P("dp", "mp"), P("dp", "mp"))
    return jax.shard_map(
        on_device, mesh=mesh, in_specs=in_specs, out_specs=out_specs, check_vma=False
    )
```

```python
import math

import jax
import jax.numpy as jnp
from jax import lax
from jax.experimental import pallas as pl
from jax.experimental.pallas import tpu as pltpu
from jax.sharding import PartitionSpec as P

CAPACITY = 2
CORES = 2
EXTRA = 128
BLOCKS = 4
SCORE_SCALE = 80.0
GRADIENT_SCALE = 2560.0
EPSILON = 1e-06
LAST_BOTH = (((1,), (1,)), ((), ()))
FIRST_BOTH = (((0,), (0,)), ((), ()))
F32 = jnp.float32
BF16 = jnp.bfloat16


def dot(a, b, dims=(((1,), (0,)), ((), ()))):
    return lax.dot_general(a, b, dims, preferred_element_type=F32)


def swap(x, axis, groups=None):
    return lax.all_to_all(
        x, axis, split_axis=0, concat_axis=0, tiled=True, axis_index_groups=groups
    )


def from_all(x, axis):
    return swap(jnp.broadcast_to(x[None], (lax.axis_size(axis),) + x.shape), axis)


def sum_all(x, axis):
    return jnp.sum(from_all(x, axis), axis=0)


def parts_of(x, count):
    out = []
    for _ in range(count):
        part = lax.reduce_precision(x, 8, 7)
        out.append(part.astype(BF16))
        x = x - part
    return out


def columns(parts):
    stacked = jnp.stack(parts, axis=1)
    return jnp.pad(stacked, ((0, 0), (0, EXTRA - len(parts))))


def lines(shards, parts):
    side = math.isqrt(shards // CORES)

    def shard(z, y, core):
        return (z * side + y) * CORES + core

    first = [
        [shard(z, y, 0) * parts + m for m in range(parts) for y in range(side)]
        for z in range(side)
    ] + [
        [shard(z, y, 1) * parts + m for m in range(parts) for z in range(side)]
        for y in range(side)
    ]

    def swaps(odd):
        partner = [((p + odd) ^ 1) - odd for p in range(side)]
        partner = [p % side for p in partner]
        out = []
        for z in range(side):
            for y in range(side):
                out.append((shard(z, y, 0), shard(partner[z], y, 0)))
                out.append((shard(z, y, 1), shard(z, partner[y], 1)))
        return out

    other_core = [(d, d ^ 1) for d in range(shards)]
    return side, first, (swaps(0), swaps(1)), other_core


def project_kernel(places, states, *refs):
    groups = len(refs[:-5]) // BLOCKS
    blocks = refs[: groups * BLOCKS]
    weight_out, projected, squares, weight, sems = refs[groups * BLOCKS :]
    rows = blocks[0].shape[0]
    tile = rows * BLOCKS

    def base(group):
        return pl.multiple_of(places[group] * tile, tile)

    copies = []
    for i, block in enumerate(blocks):
        at = pl.multiple_of(base(i // BLOCKS) + places[groups + i] * rows, rows)
        copies.append(pltpu.make_async_copy(block, weight.at[pl.ds(at, rows)], sems.at[i]))
        copies[-1].start()
    total = jnp.zeros(squares.shape, F32)
    outs = []
    for group in range(groups):
        for copy in copies[group * BLOCKS : (group + 1) * BLOCKS]:
            copy.wait()
        at = pl.ds(base(group), tile)
        outs.append(
            pltpu.make_async_copy(
                weight.at[at], weight_out.at[at], sems.at[groups * BLOCKS + group]
            )
        )
        outs[-1].start()
        value = dot(states[...], weight[at, :], LAST_BOTH)
        projected[:, at] = value
        total = total + jnp.sum(value * value, axis=1, keepdims=True)
    squares[...] = total
    for out in outs:
        out.wait()


def project(places, states, blocks):
    rows, depth = states.shape
    width = sum(block.shape[0] for block in blocks)
    vmem = pl.BlockSpec(memory_space=pltpu.VMEM)
    anywhere = pl.BlockSpec(memory_space=pl.ANY)
    return pl.pallas_call(
        project_kernel,
        out_shape=(
            jax.ShapeDtypeStruct((width, depth), BF16),
            jax.ShapeDtypeStruct((rows, width), F32),
            jax.ShapeDtypeStruct((rows, 1), F32),
        ),
        in_specs=[pl.BlockSpec(memory_space=pltpu.SMEM), vmem] + [anywhere] * len(blocks),
        out_specs=(anywhere, vmem, vmem),
        scratch_shapes=[
            pltpu.VMEM((width, depth), BF16),
            pltpu.SemaphoreType.DMA((len(blocks) + len(blocks) // BLOCKS,)),
        ],
        compiler_params=pltpu.CompilerParams(vmem_limit_bytes=24 * 2**20),
        cost_estimate=pl.CostEstimate(
            flops=2 * rows * depth * width,
            bytes_accessed=4 * width * depth,
            transcendentals=0,
        ),
    )(places, states, *blocks)


def spread_kernel(grad, weight, out):
    out[0] = dot(grad[...], weight[...]).astype(BF16)


def spread(grad, weight, parts):
    rows, width = grad.shape
    columns_each = weight.shape[1] // parts
    tile = min(512, columns_each)
    per_part = columns_each // tile
    return pl.pallas_call(
        spread_kernel,
        grid=(parts * per_part,),
        out_shape=jax.ShapeDtypeStruct((parts, rows, columns_each), BF16),
        in_specs=[
            pl.BlockSpec((rows, width), lambda n: (0, 0)),
            pl.BlockSpec((width, tile), lambda n: (0, n)),
        ],
        out_specs=pl.BlockSpec((1, rows, tile), lambda n: (n // per_part, 0, n % per_part)),
        compiler_params=pltpu.CompilerParams(vmem_limit_bytes=24 * 2**20),
        cost_estimate=pl.CostEstimate(
            flops=2 * rows * width * weight.shape[1],
            bytes_accessed=2 * width * weight.shape[1],
            transcendentals=0,
        ),
    )(grad, weight)


def on_device(query_states, passage_states, head_weight, positives, negatives):
    pairs, width = query_states.shape
    parts = lax.axis_size("mp")
    shards = lax.axis_size("dp")
    slots = shards * CAPACITY
    side, first, matchings, other_core = lines(shards, parts)
    rows = head_weight.shape[0] // parts
    shard = lax.axis_index("dp")
    core = shard % CORES
    z, y = shard // (CORES * side), (shard // CORES) % side

    line = jnp.broadcast_to(
        head_weight.reshape(parts, 1, rows, width), (parts, side, rows, width)
    ).reshape(parts * side, rows, width)
    line = swap(line, ("dp", "mp"), first).reshape(parts, side, rows, width)
    line = line.transpose(1, 2, 0, 3).reshape(side * rows, parts * width)

    position = jnp.where(core == 0, z, y)
    halves = (line[: side * rows // 2], line[side * rows // 2 :])
    own_blocks = [], []
    held = list(halves)
    for step in range(BLOCKS):
        for stream in range(2):
            came = lax.ppermute(held[stream], "dp", matchings[(step + stream) % 2])
            if step == 0:
                is_lower = (position + stream) % 2 == 0
                half = halves[stream]
                came = jnp.concatenate(
                    [jnp.where(is_lower, half, came), jnp.where(is_lower, came, half)], axis=0
                )
            own_blocks[stream].append(came)
            held[stream] = came
    own_blocks = own_blocks[0] + own_blocks[1]
    other_blocks = [lax.ppermute(block, "dp", other_core) for block in own_blocks]

    def places_of(core, position):
        groups, places = [], []
        for stream in range(2):
            groups.append(core * 2 + stream)
            up = (position + stream) % 2
            index = (position + stream) // 2
            for move in (0, 2 * up - 1, 1 - 2 * up, 2):
                places.append((index + move) % BLOCKS)
        return groups, places

    own_groups, own_places = places_of(core, position)
    other_groups, other_places = places_of(1 - core, jnp.where(core == 0, y, z))
    places = jnp.stack(own_groups + other_groups + own_places + other_places).astype(jnp.int32)

    states = jnp.concatenate([query_states, passage_states], axis=0)
    me = lax.axis_index("mp")
    came = [states] + [
        lax.ppermute(states, "mp", [(i, (i + k) % parts) for i in range(parts)])
        for k in range(1, parts)
    ]
    came = jnp.stack(came)
    states = jnp.concatenate(
        [lax.dynamic_index_in_dim(came, (me - m) % parts, 0, False) for m in range(parts)],
        axis=1,
    )

    block = negatives.reshape(-1)
    order = jnp.arange(pairs, dtype=jnp.int32)
    earlier = (block[:, None] == block[None, :]) & (order[None, :] < order[:, None])
    slot = block * CAPACITY + jnp.sum(earlier.astype(jnp.int32), axis=1)
    in_slot = jnp.arange(slots, dtype=jnp.int32)[:, None] == slot[None, :]
    to_slot = in_slot.astype(BF16)
    positive_mask = (positives[:, None] == order[None, :]).astype(F32)

    weight, projected, squares = project(places, states, own_blocks + other_blocks)
    squares = sum_all(squares.reshape(-1, math.gcd(128, 2 * pairs)), "mp").reshape(-1)
    inverse = lax.rsqrt(squares[:, None] + EPSILON)
    embedded = (projected * inverse).astype(BF16)
    query, passage = embedded[:pairs], embedded[pairs:]
    part = query.shape[1]

    local_scores = sum_all(dot(query, passage, LAST_BOTH), "mp")
    local_exp = jnp.exp(SCORE_SCALE * local_scores)
    local_totals = jnp.sum(local_exp, axis=1)

    def exchange(message):
        message = message.reshape(shards, CAPACITY, part + EXTRA)
        return swap(message, "dp").reshape(slots, part + EXTRA)

    outgoing = jnp.concatenate([query, columns(parts_of(local_totals, 3))], axis=1)
    arrived = exchange(dot(to_slot, outgoing).astype(BF16))
    slot_totals = jnp.sum(arrived[:, part : part + 3].astype(F32), axis=1)
    arrived = arrived[:, :part]

    hard_scores = sum_all(dot(arrived, passage, LAST_BOTH), "mp")
    hard_exp = jnp.exp(SCORE_SCALE * hard_scores)
    hard_totals = jnp.sum(hard_exp, axis=1)
    scale = GRADIENT_SCALE / (slot_totals + hard_totals)
    rounded_exp = hard_exp.astype(BF16)
    hard_radial = scale * jnp.sum(rounded_exp.astype(F32) * hard_scores, axis=1)
    hard_sums = (scale[:, None] * dot(rounded_exp, passage)).astype(BF16)
    back = columns(parts_of(hard_totals, 3) + parts_of(hard_radial, 3))
    back = exchange(jnp.concatenate([hard_sums, back], axis=1))
    back = dot(to_slot, back, FIRST_BOTH)
    hard_coef = (hard_exp * scale[:, None]).astype(BF16)

    totals = local_totals + jnp.sum(back[:, part : part + 3], axis=1)
    local_coef = (
        GRADIENT_SCALE * (local_exp / totals[:, None] - positive_mask)
    ).astype(BF16)
    weighted_scores = local_coef.astype(F32) * local_scores

    query_grad = dot(local_coef, passage) + back[:, :part]
    query_radial = jnp.sum(weighted_scores, axis=1) + jnp.sum(
        back[:, part + 3 : part + 6], axis=1
    )
    passage_grad = dot(local_coef, query, FIRST_BOTH) + dot(hard_coef, arrived, FIRST_BOTH)
    passage_radial = jnp.sum(weighted_scores, axis=0) + jnp.sum(
        hard_coef.astype(F32) * hard_scores, axis=0
    )
    grad = jnp.concatenate([query_grad, passage_grad], axis=0)
    radial = jnp.concatenate([query_radial, passage_radial], axis=0)[:, None]
    proj_grad = (inverse * grad - projected * (inverse * inverse * radial)).astype(BF16)
    partial = spread(proj_grad, weight, parts)
    state_grad = jnp.sum(swap(partial, "mp").astype(F32), axis=0)
    return (state_grad[:pairs], state_grad[pairs:])


def solution(mesh):
    in_specs = (P("dp", "mp"), P("dp", "mp"), P("dp", "mp"), P("dp"), P("dp", None))
    out_specs = (P("dp", "mp"), P("dp", "mp"))
    return jax.shard_map(
        on_device, mesh=mesh, in_specs=in_specs, out_specs=out_specs, check_vma=False
    )
```

```python
import math

import jax
import jax.numpy as jnp
from jax import lax
from jax.experimental import pallas as pl
from jax.experimental.pallas import tpu as pltpu
from jax.sharding import PartitionSpec as P

CAPACITY = 2
CORES = 2
EXTRA = 128
BLOCKS = 4
SCORE_SCALE = 80.0
GRADIENT_SCALE = 2560.0
EPSILON = 1e-06
LAST_BOTH = (((1,), (1,)), ((), ()))
FIRST_BOTH = (((0,), (0,)), ((), ()))
F32 = jnp.float32
BF16 = jnp.bfloat16


def dot(a, b, dims=(((1,), (0,)), ((), ()))):
    return lax.dot_general(a, b, dims, preferred_element_type=F32)


def swap(x, axis, groups=None):
    return lax.all_to_all(
        x, axis, split_axis=0, concat_axis=0, tiled=True, axis_index_groups=groups
    )


def from_all(x, axis):
    return swap(jnp.broadcast_to(x[None], (lax.axis_size(axis),) + x.shape), axis)


def sum_all(x, axis):
    return jnp.sum(from_all(x, axis), axis=0)


def parts_of(x, count):
    out = []
    for _ in range(count):
        part = lax.reduce_precision(x, 8, 7)
        out.append(part.astype(BF16))
        x = x - part
    return out


def columns(parts):
    stacked = jnp.stack(parts, axis=1)
    return jnp.pad(stacked, ((0, 0), (0, EXTRA - len(parts))))


def lines(shards, parts):
    side = math.isqrt(shards // CORES)

    def shard(z, y, core):
        return (z * side + y) * CORES + core

    first = [
        [shard(z, y, 0) * parts + m for m in range(parts) for y in range(side)]
        for z in range(side)
    ] + [
        [shard(z, y, 1) * parts + m for m in range(parts) for z in range(side)]
        for y in range(side)
    ]

    def swaps(odd):
        partner = [((p + odd) ^ 1) - odd for p in range(side)]
        partner = [p % side for p in partner]
        out = []
        for z in range(side):
            for y in range(side):
                out.append((shard(z, y, 0), shard(partner[z], y, 0)))
                out.append((shard(z, y, 1), shard(z, partner[y], 1)))
        return out

    other_core = [(d, d ^ 1) for d in range(shards)]
    return side, first, (swaps(0), swaps(1)), other_core


def project_kernel(places, states, *refs):
    arrays, (weight_out, projected, squares, weight, sems) = refs[:-5], refs[-5:]
    rows = weight.shape[0] // (2 * BLOCKS)
    tile, width = rows * BLOCKS, states.shape[2]
    copies, count = ([], []), 0
    for array, streams in zip(arrays, block_streams(len(arrays))):
        for i, stream in enumerate(streams):
            at = pl.multiple_of(stream * tile + places[count] * rows, rows)
            copy = pltpu.make_async_copy(
                array.at[pl.ds(i * rows, rows)], weight.at[pl.ds(at, rows)], sems.at[count]
            )
            copy.start()
            copies[stream].append(copy)
            count += 1
    total = jnp.zeros(squares.shape, F32)
    outs = []
    for stream in range(2):
        for copy in copies[stream]:
            copy.wait()
        at = pl.ds(stream * tile, tile)
        outs.append(
            pltpu.make_async_copy(weight.at[at], weight_out.at[at], sems.at[count + stream])
        )
        outs[-1].start()
        value = dot(states[0], weight[at, :width], LAST_BOTH)
        for part in range(1, states.shape[0]):
            columns_at = pl.ds(part * width, width)
            value = value + dot(states[part], weight[at, columns_at], LAST_BOTH)
        projected[:, at] = value
        total = total + jnp.sum(value * value, axis=1, keepdims=True)
    squares[...] = total
    for out in outs:
        out.wait()


def block_streams(arrays):
    return [[0], [1]] * BLOCKS


def project(places, states, arrays):
    parts, rows, each = states.shape
    depth = parts * each
    width = sum(array.shape[0] for array in arrays)
    vmem = pl.BlockSpec(memory_space=pltpu.VMEM)
    return pl.pallas_call(
        project_kernel,
        out_shape=(
            jax.ShapeDtypeStruct((width, depth), BF16),
            jax.ShapeDtypeStruct((rows, width), F32),
            jax.ShapeDtypeStruct((rows, 1), F32),
        ),
        in_specs=[pl.BlockSpec(memory_space=pltpu.SMEM), vmem]
        + [pl.BlockSpec(memory_space=pl.ANY)] * len(arrays),
        out_specs=(pl.BlockSpec(memory_space=pltpu.HBM), vmem, vmem),
        scratch_shapes=[
            pltpu.VMEM((width, depth), BF16),
            pltpu.SemaphoreType.DMA((2 * BLOCKS + 2,)),
        ],
        compiler_params=pltpu.CompilerParams(vmem_limit_bytes=52 * 2**20),
        cost_estimate=pl.CostEstimate(
            flops=2 * rows * depth * width,
            bytes_accessed=4 * width * depth,
            transcendentals=0,
        ),
    )(places, states, *arrays)


def spread_kernel(grad_own, grad_other, weight_own, weight_other, out):
    value = dot(grad_own[...], weight_own[...]) + dot(grad_other[...], weight_other[...])
    out[0] = value.astype(BF16)


def spread(grad_own, grad_other, weight_own, weight_other, parts):
    rows, width = grad_own.shape
    columns_each = weight_own.shape[1] // parts
    tile = min(512, columns_each)
    per_part = columns_each // tile
    return pl.pallas_call(
        spread_kernel,
        grid=(parts * per_part,),
        out_shape=jax.ShapeDtypeStruct((parts, rows, columns_each), BF16),
        in_specs=[pl.BlockSpec((rows, width), lambda n: (0, 0))] * 2
        + [pl.BlockSpec((width, tile), lambda n: (0, n))] * 2,
        out_specs=pl.BlockSpec((1, rows, tile), lambda n: (n // per_part, 0, n % per_part)),
        compiler_params=pltpu.CompilerParams(vmem_limit_bytes=24 * 2**20),
        cost_estimate=pl.CostEstimate(
            flops=4 * rows * width * weight_own.shape[1],
            bytes_accessed=4 * width * weight_own.shape[1],
            transcendentals=0,
        ),
    )(grad_own, grad_other, weight_own, weight_other)


def on_device(query_states, passage_states, head_weight, positives, negatives):
    pairs, width = query_states.shape
    parts = lax.axis_size("mp")
    shards = lax.axis_size("dp")
    side, first, matchings, other_core = lines(shards, parts)
    rows = head_weight.shape[0] // parts
    shard = lax.axis_index("dp")
    core = shard % CORES
    z, y = shard // (CORES * side), (shard // CORES) % side

    line = jnp.broadcast_to(
        head_weight.reshape(parts, 1, rows, width), (parts, side, rows, width)
    ).reshape(parts * side, rows, width)
    line = swap(line, ("dp", "mp"), first).reshape(parts, side, rows, width)
    line = line.transpose(1, 2, 0, 3).reshape(side * rows, parts * width)

    position = jnp.where(core == 0, z, y)
    halves = (line[: side * rows // 2], line[side * rows // 2 :])
    states = jnp.concatenate([query_states, passage_states], axis=0)
    states, *halves = lax.optimization_barrier((states, *halves))
    states = from_all(states, "mp")
    own_blocks = [], []
    other_arrays = []
    held = halves
    for step in range(BLOCKS):
        came = [
            lax.ppermute(held[stream], "dp", matchings[(step + stream) % 2])
            for stream in range(2)
        ]
        if step == 0:
            came = lax.optimization_barrier(came)
            for stream in range(2):
                is_lower = (position + stream) % 2 == 0
                half, other = halves[stream], came[stream]
                came[stream] = jnp.concatenate(
                    [jnp.where(is_lower, half, other), jnp.where(is_lower, other, half)], axis=0
                )
        else:
            (*came, other_arrays) = lax.optimization_barrier((*came, other_arrays))
            other_arrays += [lax.ppermute(block, "dp", other_core) for block in held]
        for stream in range(2):
            own_blocks[stream].append(came[stream])
        held = came
    other_arrays += [lax.ppermute(block, "dp", other_core) for block in held]
    own_arrays = [blocks[step] for step in range(BLOCKS) for blocks in own_blocks]

    def places_of(position):
        out = []
        for move in (lambda up: 0, lambda up: 2 * up - 1, lambda up: 1 - 2 * up, lambda up: 2):
            for stream in range(2):
                at = position + stream
                out.append((at // 2 + move(at % 2)) % BLOCKS)
        return jnp.stack(out).astype(jnp.int32)

    own_places = places_of(position)
    other_places = places_of(jnp.where(core == 0, y, z))

    block = negatives.reshape(-1)
    order = jnp.arange(pairs, dtype=jnp.int32)
    earlier = (block[:, None] == block[None, :]) & (order[None, :] < order[:, None])
    slot = block * CAPACITY + jnp.sum(earlier.astype(jnp.int32), axis=1)
    slots = shards * CAPACITY
    in_slot = jnp.arange(slots, dtype=jnp.int32)[:, None] == slot[None, :]
    to_slot = in_slot.astype(BF16)
    positive_mask = (positives[:, None] == order[None, :]).astype(F32)

    def in_order(own, other):
        return jnp.where(core == 0, own, other), jnp.where(core == 0, other, own)

    weight_own, projected_own, squares = project(own_places, states, own_arrays)
    weight_other, projected_other, more = project(other_places, states, other_arrays)
    squares = squares + more
    projected = jnp.concatenate(in_order(projected_own, projected_other), axis=1)
    squares = sum_all(squares.reshape(-1, math.gcd(128, 2 * pairs)), "mp").reshape(-1)
    inverse = lax.rsqrt(squares[:, None] + EPSILON)
    embedded = (projected * inverse).astype(BF16)
    query, passage = embedded[:pairs], embedded[pairs:]
    part = query.shape[1]

    def exchange(message):
        columns_each = message.shape[1]
        message = message.reshape(shards, CAPACITY, columns_each)
        return swap(message, "dp").reshape(slots, columns_each)

    arrived = exchange(dot(to_slot, query).astype(BF16))

    scores = jnp.concatenate([arrived, query], axis=0)
    scores = sum_all(dot(scores, passage, LAST_BOTH), "mp")
    exps = jnp.exp(SCORE_SCALE * scores)
    hard_scores, local_scores = scores[:slots], scores[slots:]
    hard_exp, local_exp = exps[:slots], exps[slots:]
    sums = jnp.sum(exps, axis=1)
    hard_totals, local_totals = sums[:slots], sums[slots:]

    scale = GRADIENT_SCALE / hard_totals
    rounded_exp = hard_exp.astype(BF16)
    hard_radial = jnp.sum(rounded_exp.astype(F32) * hard_scores, axis=1) * scale
    hard_sums = (scale[:, None] * dot(rounded_exp, passage)).astype(BF16)
    totals_out = jnp.sum(jnp.where(in_slot, local_totals[None, :], 0.0), axis=1)
    back = columns(parts_of(hard_totals, 3) + parts_of(hard_radial, 3) + parts_of(totals_out, 3))
    back = exchange(jnp.concatenate([hard_sums, back], axis=1))
    slot_totals = jnp.sum(back[:, part + 6 : part + 9].astype(F32), axis=1) + hard_totals
    back = dot(to_slot, back, FIRST_BOTH)
    hard_coef = ((GRADIENT_SCALE * hard_exp) / slot_totals[:, None]).astype(BF16)

    query_hard_totals = jnp.sum(back[:, part : part + 3], axis=1)
    totals = local_totals + query_hard_totals
    share = (query_hard_totals / totals)[:, None]
    local_coef = (
        GRADIENT_SCALE * (local_exp / totals[:, None] - positive_mask)
    ).astype(BF16)
    weighted_scores = local_coef.astype(F32) * local_scores

    query_grad = dot(local_coef, passage) + share * back[:, :part]
    query_radial = jnp.sum(weighted_scores, axis=1) + share[:, 0] * jnp.sum(
        back[:, part + 3 : part + 6], axis=1
    )
    passage_grad = dot(local_coef, query, FIRST_BOTH) + dot(hard_coef, arrived, FIRST_BOTH)
    passage_radial = jnp.sum(weighted_scores, axis=0) + jnp.sum(
        hard_coef.astype(F32) * hard_scores, axis=0
    )
    grad = jnp.concatenate([query_grad, passage_grad], axis=0)
    radial = jnp.concatenate([query_radial, passage_radial], axis=0)[:, None]
    proj_grad = (inverse * grad - projected * (inverse * inverse * radial)).astype(BF16)
    half = part // 2
    grad_own, grad_other = in_order(proj_grad[:, :half], proj_grad[:, half:])
    partial = spread(grad_own, grad_other, weight_own, weight_other, parts)
    state_grad = jnp.sum(swap(partial, "mp").astype(F32), axis=0)
    return (state_grad[:pairs], state_grad[pairs:])


def solution(mesh):
    in_specs = (P("dp", "mp"), P("dp", "mp"), P("dp", "mp"), P("dp"), P("dp", None))
    out_specs = (P("dp", "mp"), P("dp", "mp"))
    return jax.shard_map(
        on_device, mesh=mesh, in_specs=in_specs, out_specs=out_specs, check_vma=False
    )
```

```python
import math

import jax
import jax.numpy as jnp
from jax import lax
from jax.experimental import pallas as pl
from jax.experimental.pallas import tpu as pltpu
from jax.sharding import PartitionSpec as P

CAPACITY = 2
CORES = 2
EXTRA = 128
BLOCKS = 4
SCORE_SCALE = 80.0
GRADIENT_SCALE = 2560.0
EPSILON = 1e-06
LAST_BOTH = (((1,), (1,)), ((), ()))
FIRST_BOTH = (((0,), (0,)), ((), ()))
F32 = jnp.float32
BF16 = jnp.bfloat16


def dot(a, b, dims=(((1,), (0,)), ((), ()))):
    return lax.dot_general(a, b, dims, preferred_element_type=F32)


def swap(x, axis, groups=None):
    return lax.all_to_all(
        x, axis, split_axis=0, concat_axis=0, tiled=True, axis_index_groups=groups
    )


def from_all(x, axis):
    return swap(jnp.broadcast_to(x[None], (lax.axis_size(axis),) + x.shape), axis)


def sum_all(x, axis):
    return jnp.sum(from_all(x, axis), axis=0)


def parts_of(x, count):
    out = []
    for _ in range(count):
        part = lax.reduce_precision(x, 8, 7)
        out.append(part.astype(BF16))
        x = x - part
    return out


def columns(parts):
    stacked = jnp.stack(parts, axis=1)
    return jnp.pad(stacked, ((0, 0), (0, EXTRA - len(parts))))


def lines(shards, parts):
    side = math.isqrt(shards // CORES)

    def shard(z, y, core):
        return (z * side + y) * CORES + core

    first = [
        [shard(z, y, 0) * parts + m for m in range(parts) for y in range(side)]
        for z in range(side)
    ] + [
        [shard(z, y, 1) * parts + m for m in range(parts) for z in range(side)]
        for y in range(side)
    ]

    def swaps(odd):
        partner = [((p + odd) ^ 1) - odd for p in range(side)]
        partner = [p % side for p in partner]
        out = []
        for z in range(side):
            for y in range(side):
                out.append((shard(z, y, 0), shard(partner[z], y, 0)))
                out.append((shard(z, y, 1), shard(z, partner[y], 1)))
        return out

    other_core = [(d, d ^ 1) for d in range(shards)]
    return side, first, (swaps(0), swaps(1)), other_core


def place_kernel(places, *refs):
    blocks, (weight, sems) = refs[:-2], refs[-2:]
    rows = blocks[0].shape[0]
    copies = []
    for i, block in enumerate(blocks):
        at = pl.multiple_of(places[i] * rows, rows)
        copies.append(pltpu.make_async_copy(block, weight.at[pl.ds(at, rows)], sems.at[i]))
        copies[-1].start()
    for copy in copies:
        copy.wait()


def place(places, blocks):
    rows, depth = blocks[0].shape
    anywhere = pl.BlockSpec(memory_space=pl.ANY)
    return pl.pallas_call(
        place_kernel,
        out_shape=jax.ShapeDtypeStruct((len(blocks) * rows, depth), BF16),
        in_specs=[pl.BlockSpec(memory_space=pltpu.SMEM)] + [anywhere] * len(blocks),
        out_specs=pl.BlockSpec(memory_space=pltpu.VMEM),
        scratch_shapes=[pltpu.SemaphoreType.DMA((len(blocks),))],
        compiler_params=pltpu.CompilerParams(vmem_limit_bytes=16 * 2**20),
    )(places, *blocks)


def project_kernel(states, weight, projected, squares):
    value = dot(states[0], weight[:, : states.shape[2]], LAST_BOTH)
    for part in range(1, states.shape[0]):
        at = pl.ds(part * states.shape[2], states.shape[2])
        value = value + dot(states[part], weight[:, at], LAST_BOTH)
    projected[...] = value
    total = jnp.sum(value * value, axis=1, keepdims=True)

    @pl.when(pl.program_id(0) == 0)
    def _():
        squares[...] = total

    @pl.when(pl.program_id(0) > 0)
    def _():
        squares[...] += total


def project(states, weight):
    parts, rows, _ = states.shape
    width, depth = weight.shape
    tile = min(256, width)
    return pl.pallas_call(
        project_kernel,
        grid=(width // tile,),
        out_shape=(
            jax.ShapeDtypeStruct((rows, width), F32),
            jax.ShapeDtypeStruct((rows, 1), F32),
        ),
        in_specs=[
            pl.BlockSpec(states.shape, lambda n: (0, 0, 0)),
            pl.BlockSpec((tile, depth), lambda n: (n, 0)),
        ],
        out_specs=(
            pl.BlockSpec((rows, tile), lambda n: (0, n)),
            pl.BlockSpec((rows, 1), lambda n: (0, 0)),
        ),
        compiler_params=pltpu.CompilerParams(vmem_limit_bytes=24 * 2**20),
        cost_estimate=pl.CostEstimate(
            flops=2 * rows * depth * width,
            bytes_accessed=2 * width * depth,
            transcendentals=0,
        ),
    )(states, weight)


def spread_kernel(grad_own, grad_other, weight_own, weight_other, out):
    value = dot(grad_own[...], weight_own[...]) + dot(grad_other[...], weight_other[...])
    out[0] = value.astype(BF16)


def spread(grad_own, grad_other, weight_own, weight_other, parts):
    rows, width = grad_own.shape
    columns_each = weight_own.shape[1] // parts
    tile = min(1024, columns_each)
    per_part = columns_each // tile
    return pl.pallas_call(
        spread_kernel,
        grid=(parts * per_part,),
        out_shape=jax.ShapeDtypeStruct((parts, rows, columns_each), BF16),
        in_specs=[pl.BlockSpec((rows, width), lambda n: (0, 0))] * 2
        + [pl.BlockSpec((width, tile), lambda n: (0, n))] * 2,
        out_specs=pl.BlockSpec((1, rows, tile), lambda n: (n // per_part, 0, n % per_part)),
        compiler_params=pltpu.CompilerParams(vmem_limit_bytes=24 * 2**20),
        cost_estimate=pl.CostEstimate(
            flops=4 * rows * width * weight_own.shape[1],
            bytes_accessed=4 * width * weight_own.shape[1],
            transcendentals=0,
        ),
    )(grad_own, grad_other, weight_own, weight_other)


def on_device(query_states, passage_states, head_weight, positives, negatives):
    pairs, width = query_states.shape
    parts = lax.axis_size("mp")
    shards = lax.axis_size("dp")
    side, first, matchings, other_core = lines(shards, parts)
    rows = head_weight.shape[0] // parts
    shard = lax.axis_index("dp")
    core = shard % CORES
    z, y = shard // (CORES * side), (shard // CORES) % side

    line = jnp.broadcast_to(
        head_weight.reshape(parts, 1, rows, width), (parts, side, rows, width)
    ).reshape(parts * side, rows, width)
    line = swap(line, ("dp", "mp"), first).reshape(parts, side, rows, width)
    line = line.transpose(1, 2, 0, 3).reshape(side * rows, parts * width)

    position = jnp.where(core == 0, z, y)
    halves = (line[: side * rows // 2], line[side * rows // 2 :])
    states = jnp.concatenate([query_states, passage_states], axis=0)
    states, *halves = lax.optimization_barrier((states, *halves))
    states = from_all(states, "mp")
    blocks, places = [], []
    held = halves
    for step in range(BLOCKS):
        came = [
            lax.ppermute(held[stream], "dp", matchings[(step + stream) % 2])
            for stream in range(2)
        ]
        if step < BLOCKS - 1:
            came = lax.optimization_barrier(came)
        else:
            (*came, states) = lax.optimization_barrier((*came, states))
        for stream in range(2):
            at, is_upper = (position + stream) // 2, (position + stream) % 2
            if step == 0:
                half, other = halves[stream], came[stream]
                came[stream] = jnp.concatenate(
                    [jnp.where(is_upper, other, half), jnp.where(is_upper, half, other)], axis=0
                )
            move = (0, 2 * is_upper - 1, 1 - 2 * is_upper, 2)[step]
            places.append(stream * BLOCKS + (at + move) % BLOCKS)
        blocks += came
        held = came
    weight_own = place(jnp.stack(places).astype(jnp.int32), blocks)
    weight_other = lax.ppermute(weight_own, "dp", other_core)

    block = negatives.reshape(-1)
    order = jnp.arange(pairs, dtype=jnp.int32)
    earlier = (block[:, None] == block[None, :]) & (order[None, :] < order[:, None])
    slot = block * CAPACITY + jnp.sum(earlier.astype(jnp.int32), axis=1)
    slots = shards * CAPACITY
    in_slot = jnp.arange(slots, dtype=jnp.int32)[:, None] == slot[None, :]
    to_slot = in_slot.astype(BF16)
    positive_mask = (positives[:, None] == order[None, :]).astype(F32)

    def in_order(own, other):
        return jnp.where(core == 0, own, other), jnp.where(core == 0, other, own)

    projected_own, squares = project(states, weight_own)
    projected_other, more = project(states, weight_other)
    squares = squares + more
    projected = jnp.concatenate(in_order(projected_own, projected_other), axis=1)
    squares = sum_all(squares.reshape(-1, math.gcd(128, 2 * pairs)), "mp").reshape(-1)
    inverse = lax.rsqrt(squares[:, None] + EPSILON)
    embedded = (projected * inverse).astype(BF16)
    query, passage = embedded[:pairs], embedded[pairs:]
    part = query.shape[1]

    def exchange(message):
        columns_each = message.shape[1]
        message = message.reshape(shards, CAPACITY, columns_each)
        return swap(message, "dp").reshape(slots, columns_each)

    arrived = exchange(dot(to_slot, query).astype(BF16))

    scores = jnp.concatenate([arrived, query], axis=0)
    scores = sum_all(dot(scores, passage, LAST_BOTH), "mp")
    exps = jnp.exp(SCORE_SCALE * scores)
    hard_scores, local_scores = scores[:slots], scores[slots:]
    hard_exp, local_exp = exps[:slots], exps[slots:]
    sums = jnp.sum(exps, axis=1)
    hard_totals, local_totals = sums[:slots], sums[slots:]

    scale = GRADIENT_SCALE / hard_totals
    rounded_exp = hard_exp.astype(BF16)
    hard_radial = jnp.sum(rounded_exp.astype(F32) * hard_scores, axis=1) * scale
    hard_sums = (scale[:, None] * dot(rounded_exp, passage)).astype(BF16)
    totals_out = jnp.sum(jnp.where(in_slot, local_totals[None, :], 0.0), axis=1)
    back = columns(parts_of(hard_totals, 3) + parts_of(hard_radial, 3) + parts_of(totals_out, 3))
    back = exchange(jnp.concatenate([hard_sums, back], axis=1))
    slot_totals = jnp.sum(back[:, part + 6 : part + 9].astype(F32), axis=1) + hard_totals
    back = dot(to_slot, back, FIRST_BOTH)
    hard_coef = ((GRADIENT_SCALE * hard_exp) / slot_totals[:, None]).astype(BF16)

    query_hard_totals = jnp.sum(back[:, part : part + 3], axis=1)
    totals = local_totals + query_hard_totals
    share = (query_hard_totals / totals)[:, None]
    local_coef = (
        GRADIENT_SCALE * (local_exp / totals[:, None] - positive_mask)
    ).astype(BF16)
    weighted_scores = local_coef.astype(F32) * local_scores

    query_grad = dot(local_coef, passage) + share * back[:, :part]
    query_radial = jnp.sum(weighted_scores, axis=1) + share[:, 0] * jnp.sum(
        back[:, part + 3 : part + 6], axis=1
    )
    passage_grad = dot(local_coef, query, FIRST_BOTH) + dot(hard_coef, arrived, FIRST_BOTH)
    passage_radial = jnp.sum(weighted_scores, axis=0) + jnp.sum(
        hard_coef.astype(F32) * hard_scores, axis=0
    )
    grad = jnp.concatenate([query_grad, passage_grad], axis=0)
    radial = jnp.concatenate([query_radial, passage_radial], axis=0)[:, None]
    proj_grad = (inverse * grad - projected * (inverse * inverse * radial)).astype(BF16)
    half = part // 2
    grad_own, grad_other = in_order(proj_grad[:, :half], proj_grad[:, half:])
    partial = spread(grad_own, grad_other, weight_own, weight_other, parts)
    state_grad = jnp.sum(swap(partial, "mp").astype(F32), axis=0)
    return (state_grad[:pairs], state_grad[pairs:])


def solution(mesh):
    in_specs = (P("dp", "mp"), P("dp", "mp"), P("dp", "mp"), P("dp"), P("dp", None))
    out_specs = (P("dp", "mp"), P("dp", "mp"))
    return jax.shard_map(
        on_device, mesh=mesh, in_specs=in_specs, out_specs=out_specs, check_vma=False
    )
```

```python
import math

import jax
import jax.numpy as jnp
from jax import lax
from jax.experimental import pallas as pl
from jax.experimental.pallas import tpu as pltpu
from jax.sharding import PartitionSpec as P

CAPACITY = 2
CORES = 2
EXTRA = 128
BLOCKS = 4
SCORE_SCALE = 80.0
GRADIENT_SCALE = 2560.0
EPSILON = 1e-06
LAST_BOTH = (((1,), (1,)), ((), ()))
FIRST_BOTH = (((0,), (0,)), ((), ()))
F32 = jnp.float32
BF16 = jnp.bfloat16


def dot(a, b, dims=(((1,), (0,)), ((), ()))):
    return lax.dot_general(a, b, dims, preferred_element_type=F32)


def swap(x, axis, groups=None):
    return lax.all_to_all(
        x, axis, split_axis=0, concat_axis=0, tiled=True, axis_index_groups=groups
    )


def from_all(x, axis):
    return swap(jnp.broadcast_to(x[None], (lax.axis_size(axis),) + x.shape), axis)


def sum_all(x, axis):
    return jnp.sum(from_all(x, axis), axis=0)


def parts_of(x, count):
    out = []
    for _ in range(count):
        part = lax.reduce_precision(x, 8, 7)
        out.append(part.astype(BF16))
        x = x - part
    return out


def columns(parts):
    stacked = jnp.stack(parts, axis=1)
    return jnp.pad(stacked, ((0, 0), (0, EXTRA - len(parts))))


def lines(shards, parts):
    side = math.isqrt(shards // CORES)

    def shard(z, y, core):
        return (z * side + y) * CORES + core

    first = [
        [shard(z, y, 0) * parts + m for m in range(parts) for y in range(side)]
        for z in range(side)
    ] + [
        [shard(z, y, 1) * parts + m for m in range(parts) for z in range(side)]
        for y in range(side)
    ]

    def swaps(odd):
        partner = [((p + odd) ^ 1) - odd for p in range(side)]
        partner = [p % side for p in partner]
        out = []
        for z in range(side):
            for y in range(side):
                out.append((shard(z, y, 0), shard(partner[z], y, 0)))
                out.append((shard(z, y, 1), shard(z, partner[y], 1)))
        return out

    other_core = [(d, d ^ 1) for d in range(shards)]
    return side, first, (swaps(0), swaps(1)), other_core


def place_kernel(places, *refs):
    blocks, (weight, sems) = refs[:-2], refs[-2:]
    rows = blocks[0].shape[0]
    copies = []
    for i, block in enumerate(blocks):
        at = pl.multiple_of(places[i] * rows, rows)
        copies.append(pltpu.make_async_copy(block, weight.at[pl.ds(at, rows)], sems.at[i]))
        copies[-1].start()
    for copy in copies:
        copy.wait()


def place(places, blocks):
    rows, depth = blocks[0].shape
    anywhere = pl.BlockSpec(memory_space=pl.ANY)
    return pl.pallas_call(
        place_kernel,
        out_shape=jax.ShapeDtypeStruct((len(blocks) * rows, depth), BF16),
        in_specs=[pl.BlockSpec(memory_space=pltpu.SMEM)] + [anywhere] * len(blocks),
        out_specs=pl.BlockSpec(memory_space=pltpu.VMEM),
        scratch_shapes=[pltpu.SemaphoreType.DMA((len(blocks),))],
        compiler_params=pltpu.CompilerParams(vmem_limit_bytes=16 * 2**20),
    )(places, *blocks)


def project_kernel(states, weight, projected, squares):
    value = dot(states[0], weight[:, : states.shape[2]], LAST_BOTH)
    for part in range(1, states.shape[0]):
        at = pl.ds(part * states.shape[2], states.shape[2])
        value = value + dot(states[part], weight[:, at], LAST_BOTH)
    projected[...] = value
    total = jnp.sum(value * value, axis=1, keepdims=True)

    @pl.when(pl.program_id(0) == 0)
    def _():
        squares[...] = total

    @pl.when(pl.program_id(0) > 0)
    def _():
        squares[...] += total


def project(states, weight):
    parts, rows, _ = states.shape
    width, depth = weight.shape
    tile = min(256, width)
    return pl.pallas_call(
        project_kernel,
        grid=(width // tile,),
        out_shape=(
            jax.ShapeDtypeStruct((rows, width), F32),
            jax.ShapeDtypeStruct((rows, 1), F32),
        ),
        in_specs=[
            pl.BlockSpec(states.shape, lambda n: (0, 0, 0)),
            pl.BlockSpec((tile, depth), lambda n: (n, 0)),
        ],
        out_specs=(
            pl.BlockSpec((rows, tile), lambda n: (0, n)),
            pl.BlockSpec((rows, 1), lambda n: (0, 0)),
        ),
        compiler_params=pltpu.CompilerParams(vmem_limit_bytes=24 * 2**20),
        cost_estimate=pl.CostEstimate(
            flops=2 * rows * depth * width,
            bytes_accessed=2 * width * depth,
            transcendentals=0,
        ),
    )(states, weight)


def spread_kernel(grad_own, grad_other, *refs):
    weights, out = refs[:-1], refs[-1]
    depth = weights[0].shape[0]
    value = jnp.zeros(out.shape[1:], F32)
    for i, weight in enumerate(weights):
        grad = (grad_own, grad_other)[i // 2]
        at = pl.ds(i % 2 * depth, depth)
        value = value + dot(grad[:, at], weight[...])
    out[0] = value.astype(BF16)


def spread(grad_own, grad_other, weights, parts):
    rows, width = grad_own.shape
    depth, columns_all = weights[0].shape
    columns_each = columns_all // parts
    tile = min(1024, columns_each)
    per_part = columns_each // tile
    return pl.pallas_call(
        spread_kernel,
        grid=(parts * per_part,),
        out_shape=jax.ShapeDtypeStruct((parts, rows, columns_each), BF16),
        in_specs=[pl.BlockSpec((rows, width), lambda n: (0, 0))] * 2
        + [pl.BlockSpec((depth, tile), lambda n: (0, n))] * len(weights),
        out_specs=pl.BlockSpec((1, rows, tile), lambda n: (n // per_part, 0, n % per_part)),
        compiler_params=pltpu.CompilerParams(vmem_limit_bytes=24 * 2**20),
        cost_estimate=pl.CostEstimate(
            flops=4 * rows * width * columns_all,
            bytes_accessed=4 * width * columns_all,
            transcendentals=0,
        ),
    )(grad_own, grad_other, *weights)


def on_device(query_states, passage_states, head_weight, positives, negatives):
    pairs, width = query_states.shape
    parts = lax.axis_size("mp")
    shards = lax.axis_size("dp")
    side, first, matchings, other_core = lines(shards, parts)
    rows = head_weight.shape[0] // parts
    shard = lax.axis_index("dp")
    core = shard % CORES
    z, y = shard // (CORES * side), (shard // CORES) % side

    line = jnp.broadcast_to(
        head_weight.reshape(parts, 1, rows, width), (parts, side, rows, width)
    ).reshape(parts * side, rows, width)
    line = swap(line, ("dp", "mp"), first).reshape(parts, side, rows, width)
    line = line.transpose(1, 2, 0, 3).reshape(side * rows, parts * width)

    position = jnp.where(core == 0, z, y)
    halves = (line[: side * rows // 2], line[side * rows // 2 :])
    states = jnp.concatenate([query_states, passage_states], axis=0)
    states, *halves = lax.optimization_barrier((states, *halves))
    states = from_all(states, "mp")
    blocks, places = ([], []), ([], [])
    held = halves
    for step in range(BLOCKS):
        first, second = [
            lax.ppermute(held[stream], "dp", matchings[(step + stream) % 2])
            for stream in range(2)
        ]
        first, _ = lax.optimization_barrier((first, held[1]))
        if step < BLOCKS - 1:
            second, _ = lax.optimization_barrier((second, first))
        else:
            second, states, _ = lax.optimization_barrier((second, states, first))
        held = []
        for stream, came in enumerate((first, second)):
            at, is_upper = (position + stream) // 2, (position + stream) % 2
            if step == 0:
                half = halves[stream]
                came = jnp.concatenate(
                    [jnp.where(is_upper, came, half), jnp.where(is_upper, half, came)], axis=0
                )
            move = (0, 2 * is_upper - 1, 1 - 2 * is_upper, 2)[step]
            places[stream].append((at + move) % BLOCKS)
            blocks[stream].append(came)
            held.append(came)
    weights = [
        place(jnp.stack(places[stream]).astype(jnp.int32), blocks[stream]) for stream in range(2)
    ]
    weights += [lax.ppermute(weight, "dp", other_core) for weight in weights]

    block = negatives.reshape(-1)
    order = jnp.arange(pairs, dtype=jnp.int32)
    earlier = (block[:, None] == block[None, :]) & (order[None, :] < order[:, None])
    slot = block * CAPACITY + jnp.sum(earlier.astype(jnp.int32), axis=1)
    slots = shards * CAPACITY
    in_slot = jnp.arange(slots, dtype=jnp.int32)[:, None] == slot[None, :]
    to_slot = in_slot.astype(BF16)
    positive_mask = (positives[:, None] == order[None, :]).astype(F32)

    def in_order(own, other):
        return jnp.where(core == 0, own, other), jnp.where(core == 0, other, own)

    projected, squares = zip(*[project(states, weight) for weight in weights])
    squares = sum(squares)
    own, other = jnp.concatenate(projected[:2], axis=1), jnp.concatenate(projected[2:], axis=1)
    projected = jnp.concatenate(in_order(own, other), axis=1)
    squares = sum_all(squares.reshape(-1, math.gcd(128, 2 * pairs)), "mp").reshape(-1)
    inverse = lax.rsqrt(squares[:, None] + EPSILON)
    embedded = (projected * inverse).astype(BF16)
    query, passage = embedded[:pairs], embedded[pairs:]
    part = query.shape[1]

    def exchange(message):
        columns_each = message.shape[1]
        message = message.reshape(shards, CAPACITY, columns_each)
        return swap(message, "dp").reshape(slots, columns_each)

    arrived = exchange(dot(to_slot, query).astype(BF16))

    scores = jnp.concatenate([arrived, query], axis=0)
    scores = sum_all(dot(scores, passage, LAST_BOTH), "mp")
    exps = jnp.exp(SCORE_SCALE * scores)
    hard_scores, local_scores = scores[:slots], scores[slots:]
    hard_exp, local_exp = exps[:slots], exps[slots:]
    sums = jnp.sum(exps, axis=1)
    hard_totals, local_totals = sums[:slots], sums[slots:]

    scale = GRADIENT_SCALE / hard_totals
    rounded_exp = hard_exp.astype(BF16)
    hard_radial = jnp.sum(rounded_exp.astype(F32) * hard_scores, axis=1) * scale
    hard_sums = (scale[:, None] * dot(rounded_exp, passage)).astype(BF16)
    totals_out = jnp.sum(jnp.where(in_slot, local_totals[None, :], 0.0), axis=1)
    back = columns(parts_of(hard_totals, 3) + parts_of(hard_radial, 3) + parts_of(totals_out, 3))
    back = exchange(jnp.concatenate([hard_sums, back], axis=1))
    slot_totals = jnp.sum(back[:, part + 6 : part + 9].astype(F32), axis=1) + hard_totals
    back = dot(to_slot, back, FIRST_BOTH)
    hard_coef = ((GRADIENT_SCALE * hard_exp) / slot_totals[:, None]).astype(BF16)

    query_hard_totals = jnp.sum(back[:, part : part + 3], axis=1)
    totals = local_totals + query_hard_totals
    share = (query_hard_totals / totals)[:, None]
    local_coef = (
        GRADIENT_SCALE * (local_exp / totals[:, None] - positive_mask)
    ).astype(BF16)
    weighted_scores = local_coef.astype(F32) * local_scores

    query_grad = dot(local_coef, passage) + share * back[:, :part]
    query_radial = jnp.sum(weighted_scores, axis=1) + share[:, 0] * jnp.sum(
        back[:, part + 3 : part + 6], axis=1
    )
    passage_grad = dot(local_coef, query, FIRST_BOTH) + dot(hard_coef, arrived, FIRST_BOTH)
    passage_radial = jnp.sum(weighted_scores, axis=0) + jnp.sum(
        hard_coef.astype(F32) * hard_scores, axis=0
    )
    grad = jnp.concatenate([query_grad, passage_grad], axis=0)
    radial = jnp.concatenate([query_radial, passage_radial], axis=0)[:, None]
    proj_grad = (inverse * grad - projected * (inverse * inverse * radial)).astype(BF16)
    half = part // 2
    grad_own, grad_other = in_order(proj_grad[:, :half], proj_grad[:, half:])
    partial = spread(grad_own, grad_other, weights, parts)
    state_grad = jnp.sum(swap(partial, "mp").astype(F32), axis=0)
    return (state_grad[:pairs], state_grad[pairs:])


def solution(mesh):
    in_specs = (P("dp", "mp"), P("dp", "mp"), P("dp", "mp"), P("dp"), P("dp", None))
    out_specs = (P("dp", "mp"), P("dp", "mp"))
    return jax.shard_map(
        on_device, mesh=mesh, in_specs=in_specs, out_specs=out_specs, check_vma=False
    )
```

```python
import math

import jax
import jax.numpy as jnp
from jax import lax
from jax.experimental import pallas as pl
from jax.experimental.pallas import tpu as pltpu
from jax.sharding import PartitionSpec as P

CAPACITY = 2
CORES = 2
EXTRA = 128
BLOCKS = 4
SCORE_SCALE = 80.0
GRADIENT_SCALE = 2560.0
EPSILON = 1e-06
LAST_BOTH = (((1,), (1,)), ((), ()))
FIRST_BOTH = (((0,), (0,)), ((), ()))
F32 = jnp.float32
BF16 = jnp.bfloat16


def dot(a, b, dims=(((1,), (0,)), ((), ()))):
    return lax.dot_general(a, b, dims, preferred_element_type=F32)


def swap(x, axis, groups=None):
    return lax.all_to_all(
        x, axis, split_axis=0, concat_axis=0, tiled=True, axis_index_groups=groups
    )


def from_all(x, axis):
    return swap(jnp.broadcast_to(x[None], (lax.axis_size(axis),) + x.shape), axis)


def sum_all(x, axis):
    return jnp.sum(from_all(x, axis), axis=0)


def parts_of(x, count):
    out = []
    for _ in range(count):
        part = lax.reduce_precision(x, 8, 7)
        out.append(part.astype(BF16))
        x = x - part
    return out


def columns(parts):
    stacked = jnp.stack(parts, axis=1)
    return jnp.pad(stacked, ((0, 0), (0, EXTRA - len(parts))))


def lines(shards, parts):
    side = math.isqrt(shards // CORES)

    def shard(z, y, core):
        return (z * side + y) * CORES + core

    first = [
        [shard(z, y, 0) * parts + m for m in range(parts) for y in range(side)]
        for z in range(side)
    ] + [
        [shard(z, y, 1) * parts + m for m in range(parts) for z in range(side)]
        for y in range(side)
    ]

    def swaps(odd):
        partner = [((p + odd) ^ 1) - odd for p in range(side)]
        partner = [p % side for p in partner]
        out = []
        for z in range(side):
            for y in range(side):
                out.append((shard(z, y, 0), shard(partner[z], y, 0)))
                out.append((shard(z, y, 1), shard(z, partner[y], 1)))
        return out

    other_core = [(d, d ^ 1) for d in range(shards)]
    return side, first, (swaps(0), swaps(1)), other_core


def place_kernel(places, *refs):
    blocks, (weight, sems) = refs[:-2], refs[-2:]
    rows = blocks[0].shape[0]
    copies = []
    for i, block in enumerate(blocks):
        at = pl.multiple_of(places[i] * rows, rows)
        copies.append(pltpu.make_async_copy(block, weight.at[pl.ds(at, rows)], sems.at[i]))
        copies[-1].start()
    for copy in copies:
        copy.wait()


def place(places, blocks):
    rows, depth = blocks[0].shape
    anywhere = pl.BlockSpec(memory_space=pl.ANY)
    return pl.pallas_call(
        place_kernel,
        out_shape=jax.ShapeDtypeStruct((len(blocks) * rows, depth), BF16),
        in_specs=[pl.BlockSpec(memory_space=pltpu.SMEM)] + [anywhere] * len(blocks),
        out_specs=pl.BlockSpec(memory_space=pltpu.VMEM),
        scratch_shapes=[pltpu.SemaphoreType.DMA((len(blocks),))],
        compiler_params=pltpu.CompilerParams(vmem_limit_bytes=16 * 2**20),
    )(places, *blocks)


def project_kernel(states, weight, projected, squares):
    value = dot(states[0], weight[:, : states.shape[2]], LAST_BOTH)
    for part in range(1, states.shape[0]):
        at = pl.ds(part * states.shape[2], states.shape[2])
        value = value + dot(states[part], weight[:, at], LAST_BOTH)
    projected[...] = value
    total = jnp.sum(value * value, axis=1, keepdims=True)

    @pl.when(pl.program_id(0) == 0)
    def _():
        squares[...] = total

    @pl.when(pl.program_id(0) > 0)
    def _():
        squares[...] += total


def project(states, weight):
    parts, rows, _ = states.shape
    width, depth = weight.shape
    tile = min(256, width)
    return pl.pallas_call(
        project_kernel,
        grid=(width // tile,),
        out_shape=(
            jax.ShapeDtypeStruct((rows, width), F32),
            jax.ShapeDtypeStruct((rows, 1), F32),
        ),
        in_specs=[
            pl.BlockSpec(states.shape, lambda n: (0, 0, 0)),
            pl.BlockSpec((tile, depth), lambda n: (n, 0)),
        ],
        out_specs=(
            pl.BlockSpec((rows, tile), lambda n: (0, n)),
            pl.BlockSpec((rows, 1), lambda n: (0, 0)),
        ),
        compiler_params=pltpu.CompilerParams(vmem_limit_bytes=24 * 2**20),
        cost_estimate=pl.CostEstimate(
            flops=2 * rows * depth * width,
            bytes_accessed=2 * width * depth,
            transcendentals=0,
        ),
    )(states, weight)


def spread_kernel(grad_own, grad_other, *refs):
    weights, out = refs[:-1], refs[-1]
    depth = weights[0].shape[0]
    value = jnp.zeros(out.shape[1:], F32)
    for i, weight in enumerate(weights):
        grad = (grad_own, grad_other)[i // 2]
        at = pl.ds(i % 2 * depth, depth)
        value = value + dot(grad[:, at], weight[...])
    out[0] = value.astype(BF16)


def spread(grad_own, grad_other, weights, parts):
    rows, width = grad_own.shape
    depth, columns_all = weights[0].shape
    columns_each = columns_all // parts
    tile = min(1024, columns_each)
    per_part = columns_each // tile
    return pl.pallas_call(
        spread_kernel,
        grid=(parts * per_part,),
        out_shape=jax.ShapeDtypeStruct((parts, rows, columns_each), BF16),
        in_specs=[pl.BlockSpec((rows, width), lambda n: (0, 0))] * 2
        + [pl.BlockSpec((depth, tile), lambda n: (0, n))] * len(weights),
        out_specs=pl.BlockSpec((1, rows, tile), lambda n: (n // per_part, 0, n % per_part)),
        compiler_params=pltpu.CompilerParams(vmem_limit_bytes=24 * 2**20),
        cost_estimate=pl.CostEstimate(
            flops=4 * rows * width * columns_all,
            bytes_accessed=4 * width * columns_all,
            transcendentals=0,
        ),
    )(grad_own, grad_other, *weights)


def on_device(query_states, passage_states, head_weight, positives, negatives):
    pairs, width = query_states.shape
    parts = lax.axis_size("mp")
    shards = lax.axis_size("dp")
    side, first, matchings, other_core = lines(shards, parts)
    rows = head_weight.shape[0] // parts
    shard = lax.axis_index("dp")
    core = shard % CORES
    z, y = shard // (CORES * side), (shard // CORES) % side

    line = jnp.broadcast_to(
        head_weight.reshape(parts, 1, rows, width), (parts, side, rows, width)
    ).reshape(parts * side, rows, width)
    line = swap(line, ("dp", "mp"), first).reshape(parts, side, rows, width)
    line = line.transpose(1, 2, 0, 3).reshape(side * rows, parts * width)

    position = jnp.where(core == 0, z, y)
    halves = (line[: side * rows // 2], line[side * rows // 2 :])
    query_states, passage_states, *halves = lax.optimization_barrier(
        (query_states, passage_states, *halves)
    )
    states = from_all(jnp.concatenate([query_states, passage_states], axis=0), "mp")
    blocks, places = ([], []), ([], [])
    held = halves

    def placed(stream):
        return place(jnp.stack(places[stream]).astype(jnp.int32), blocks[stream])

    for step in range(BLOCKS):
        behind, ahead = [
            lax.ppermute(held[stream], "dp", matchings[(step + stream) % 2])
            for stream in range(2)
        ]
        ahead, _ = lax.optimization_barrier((ahead, held[0]))
        for stream in (1, 0):
            if stream == 0 and step < BLOCKS - 1:
                behind, _ = lax.optimization_barrier((behind, ahead))
            elif stream == 0:
                weight_ahead = placed(1)
                behind, weight_ahead, states = lax.optimization_barrier(
                    (behind, weight_ahead, states)
                )
            came = (behind, ahead)[stream]
            at, is_upper = (position + stream) // 2, (position + stream) % 2
            if step == 0:
                half = halves[stream]
                came = jnp.concatenate(
                    [jnp.where(is_upper, came, half), jnp.where(is_upper, half, came)], axis=0
                )
            move = (0, 2 * is_upper - 1, 1 - 2 * is_upper, 2)[step]
            places[stream].append((at + move) % BLOCKS)
            blocks[stream].append(came)
        held = [blocks[0][-1], blocks[1][-1]]
    weights = [placed(0), weight_ahead]
    weights += [lax.ppermute(weight, "dp", other_core) for weight in weights]

    block = negatives.reshape(-1)
    order = jnp.arange(pairs, dtype=jnp.int32)
    earlier = (block[:, None] == block[None, :]) & (order[None, :] < order[:, None])
    slot = block * CAPACITY + jnp.sum(earlier.astype(jnp.int32), axis=1)
    slots = shards * CAPACITY
    in_slot = jnp.arange(slots, dtype=jnp.int32)[:, None] == slot[None, :]
    to_slot = in_slot.astype(BF16)
    positive_mask = (positives[:, None] == order[None, :]).astype(F32)

    def in_order(own, other):
        return jnp.where(core == 0, own, other), jnp.where(core == 0, other, own)

    projected, squares = zip(*[project(states, weight) for weight in weights])
    squares = sum(squares)
    own, other = jnp.concatenate(projected[:2], axis=1), jnp.concatenate(projected[2:], axis=1)
    projected = jnp.concatenate(in_order(own, other), axis=1)
    squares = sum_all(squares.reshape(-1, math.gcd(128, 2 * pairs)), "mp").reshape(-1)
    inverse = lax.rsqrt(squares[:, None] + EPSILON)
    embedded = (projected * inverse).astype(BF16)
    query, passage = embedded[:pairs], embedded[pairs:]
    part = query.shape[1]

    def exchange(message):
        columns_each = message.shape[1]
        message = message.reshape(shards, CAPACITY, columns_each)
        return swap(message, "dp").reshape(slots, columns_each)

    outgoing, query = lax.optimization_barrier((dot(to_slot, query).astype(BF16), query))
    arrived = exchange(outgoing)

    scores = jnp.concatenate([arrived, query], axis=0)
    scores = sum_all(dot(scores, passage, LAST_BOTH), "mp")
    exps = jnp.exp(SCORE_SCALE * scores)
    hard_scores, local_scores = scores[:slots], scores[slots:]
    hard_exp, local_exp = exps[:slots], exps[slots:]
    sums = jnp.sum(exps, axis=1)
    hard_totals, local_totals = sums[:slots], sums[slots:]

    scale = GRADIENT_SCALE / hard_totals
    rounded_exp = hard_exp.astype(BF16)
    hard_radial = jnp.sum(rounded_exp.astype(F32) * hard_scores, axis=1) * scale
    hard_sums = (scale[:, None] * dot(rounded_exp, passage)).astype(BF16)
    totals_out = jnp.sum(jnp.where(in_slot, local_totals[None, :], 0.0), axis=1)
    back = columns(parts_of(hard_totals, 3) + parts_of(hard_radial, 3) + parts_of(totals_out, 3))
    back = exchange(jnp.concatenate([hard_sums, back], axis=1))
    slot_totals = jnp.sum(back[:, part + 6 : part + 9].astype(F32), axis=1) + hard_totals
    back = dot(to_slot, back, FIRST_BOTH)
    hard_coef = ((GRADIENT_SCALE * hard_exp) / slot_totals[:, None]).astype(BF16)

    query_hard_totals = jnp.sum(back[:, part : part + 3], axis=1)
    totals = local_totals + query_hard_totals
    share = (query_hard_totals / totals)[:, None]
    local_coef = (
        GRADIENT_SCALE * (local_exp / totals[:, None] - positive_mask)
    ).astype(BF16)
    weighted_scores = local_coef.astype(F32) * local_scores

    query_grad = dot(local_coef, passage) + share * back[:, :part]
    query_radial = jnp.sum(weighted_scores, axis=1) + share[:, 0] * jnp.sum(
        back[:, part + 3 : part + 6], axis=1
    )
    passage_grad = dot(local_coef, query, FIRST_BOTH) + dot(hard_coef, arrived, FIRST_BOTH)
    passage_radial = jnp.sum(weighted_scores, axis=0) + jnp.sum(
        hard_coef.astype(F32) * hard_scores, axis=0
    )
    grad = jnp.concatenate([query_grad, passage_grad], axis=0)
    radial = jnp.concatenate([query_radial, passage_radial], axis=0)[:, None]
    proj_grad = (inverse * grad - projected * (inverse * inverse * radial)).astype(BF16)
    half = part // 2
    grad_own, grad_other = in_order(proj_grad[:, :half], proj_grad[:, half:])
    partial = spread(grad_own, grad_other, weights, parts)
    state_grad = jnp.sum(swap(partial, "mp").astype(F32), axis=0)
    return (state_grad[:pairs], state_grad[pairs:])


def solution(mesh):
    in_specs = (P("dp", "mp"), P("dp", "mp"), P("dp", "mp"), P("dp"), P("dp", None))
    out_specs = (P("dp", "mp"), P("dp", "mp"))
    return jax.shard_map(
        on_device, mesh=mesh, in_specs=in_specs, out_specs=out_specs, check_vma=False
    )
```

```python
import math

import jax
import jax.numpy as jnp
from jax import lax
from jax.experimental import pallas as pl
from jax.experimental.pallas import tpu as pltpu
from jax.sharding import PartitionSpec as P

CAPACITY = 2
CORES = 2
EXTRA = 128
BLOCKS = 4
SCORE_SCALE = 80.0
GRADIENT_SCALE = 2560.0
EPSILON = 1e-06
LAST_BOTH = (((1,), (1,)), ((), ()))
FIRST_BOTH = (((0,), (0,)), ((), ()))
F32 = jnp.float32
BF16 = jnp.bfloat16


def dot(a, b, dims=(((1,), (0,)), ((), ()))):
    return lax.dot_general(a, b, dims, preferred_element_type=F32)


def swap(x, axis, groups=None):
    return lax.all_to_all(
        x, axis, split_axis=0, concat_axis=0, tiled=True, axis_index_groups=groups
    )


def from_all(x, axis):
    return swap(jnp.broadcast_to(x[None], (lax.axis_size(axis),) + x.shape), axis)


def sum_all(x, axis):
    return jnp.sum(from_all(x, axis), axis=0)


def parts_of(x, count):
    out = []
    for _ in range(count):
        part = lax.reduce_precision(x, 8, 7)
        out.append(part.astype(BF16))
        x = x - part
    return out


def columns(parts):
    stacked = jnp.stack(parts, axis=1)
    return jnp.pad(stacked, ((0, 0), (0, EXTRA - len(parts))))


def lines(shards, parts):
    side = math.isqrt(shards // CORES)

    def shard(z, y, core):
        return (z * side + y) * CORES + core

    first = [
        [shard(z, y, 0) * parts + m for m in range(parts) for y in range(side)]
        for z in range(side)
    ] + [
        [shard(z, y, 1) * parts + m for m in range(parts) for z in range(side)]
        for y in range(side)
    ]

    def swaps(odd):
        partner = [((p + odd) ^ 1) - odd for p in range(side)]
        partner = [p % side for p in partner]
        out = []
        for z in range(side):
            for y in range(side):
                out.append((shard(z, y, 0), shard(partner[z], y, 0)))
                out.append((shard(z, y, 1), shard(z, partner[y], 1)))
        return out

    other_core = [(d, d ^ 1) for d in range(shards)]
    return side, first, (swaps(0), swaps(1)), other_core


def place_kernel(places, *refs):
    blocks, (weight, sems) = refs[:-2], refs[-2:]
    rows = blocks[0].shape[0]
    copies = []
    for i, block in enumerate(blocks):
        at = pl.multiple_of(places[i] * rows, rows)
        copies.append(pltpu.make_async_copy(block, weight.at[pl.ds(at, rows)], sems.at[i]))
        copies[-1].start()
    for copy in copies:
        copy.wait()


def place(places, blocks):
    rows, depth = blocks[0].shape
    anywhere = pl.BlockSpec(memory_space=pl.ANY)
    return pl.pallas_call(
        place_kernel,
        out_shape=jax.ShapeDtypeStruct((len(blocks) * rows, depth), BF16),
        in_specs=[pl.BlockSpec(memory_space=pltpu.SMEM)] + [anywhere] * len(blocks),
        out_specs=pl.BlockSpec(memory_space=pltpu.VMEM),
        scratch_shapes=[pltpu.SemaphoreType.DMA((len(blocks),))],
        compiler_params=pltpu.CompilerParams(vmem_limit_bytes=16 * 2**20),
    )(places, *blocks)


def project_kernel(states, weight, projected, squares):
    value = dot(states[0], weight[:, : states.shape[2]], LAST_BOTH)
    for part in range(1, states.shape[0]):
        at = pl.ds(part * states.shape[2], states.shape[2])
        value = value + dot(states[part], weight[:, at], LAST_BOTH)
    projected[...] = value
    total = jnp.sum(value * value, axis=1, keepdims=True)

    @pl.when(pl.program_id(0) == 0)
    def _():
        squares[...] = total

    @pl.when(pl.program_id(0) > 0)
    def _():
        squares[...] += total


def project(states, weight):
    parts, rows, _ = states.shape
    width, depth = weight.shape
    tile = min(256, width)
    return pl.pallas_call(
        project_kernel,
        grid=(width // tile,),
        out_shape=(
            jax.ShapeDtypeStruct((rows, width), F32),
            jax.ShapeDtypeStruct((rows, 1), F32),
        ),
        in_specs=[
            pl.BlockSpec(states.shape, lambda n: (0, 0, 0)),
            pl.BlockSpec((tile, depth), lambda n: (n, 0)),
        ],
        out_specs=(
            pl.BlockSpec((rows, tile), lambda n: (0, n)),
            pl.BlockSpec((rows, 1), lambda n: (0, 0)),
        ),
        compiler_params=pltpu.CompilerParams(vmem_limit_bytes=24 * 2**20),
        cost_estimate=pl.CostEstimate(
            flops=2 * rows * depth * width,
            bytes_accessed=2 * width * depth,
            transcendentals=0,
        ),
    )(states, weight)


def spread_kernel(grad_own, grad_other, *refs):
    weights, out = refs[:-1], refs[-1]
    depth = weights[0].shape[0]
    value = jnp.zeros(out.shape[1:], F32)
    for i, weight in enumerate(weights):
        grad = (grad_own, grad_other)[i // 2]
        at = pl.ds(i % 2 * depth, depth)
        value = value + dot(grad[:, at], weight[...])
    out[0] = value.astype(BF16)


def spread(grad_own, grad_other, weights, parts):
    rows, width = grad_own.shape
    depth, columns_all = weights[0].shape
    columns_each = columns_all // parts
    tile = min(1024, columns_each)
    per_part = columns_each // tile
    return pl.pallas_call(
        spread_kernel,
        grid=(parts * per_part,),
        out_shape=jax.ShapeDtypeStruct((parts, rows, columns_each), BF16),
        in_specs=[pl.BlockSpec((rows, width), lambda n: (0, 0))] * 2
        + [pl.BlockSpec((depth, tile), lambda n: (0, n))] * len(weights),
        out_specs=pl.BlockSpec((1, rows, tile), lambda n: (n // per_part, 0, n % per_part)),
        compiler_params=pltpu.CompilerParams(vmem_limit_bytes=24 * 2**20),
        cost_estimate=pl.CostEstimate(
            flops=4 * rows * width * columns_all,
            bytes_accessed=4 * width * columns_all,
            transcendentals=0,
        ),
    )(grad_own, grad_other, *weights)


def on_device(query_states, passage_states, head_weight, positives, negatives):
    pairs, width = query_states.shape
    parts = lax.axis_size("mp")
    shards = lax.axis_size("dp")
    side, first, matchings, other_core = lines(shards, parts)
    rows = head_weight.shape[0] // parts
    shard = lax.axis_index("dp")
    core = shard % CORES
    z, y = shard // (CORES * side), (shard // CORES) % side

    line = jnp.broadcast_to(
        head_weight.reshape(parts, 1, rows, width), (parts, side, rows, width)
    ).reshape(parts * side, rows, width)
    line = swap(line, ("dp", "mp"), first).reshape(parts, side, rows, width)
    line = line.transpose(1, 2, 0, 3).reshape(side * rows, parts * width)

    position = jnp.where(core == 0, z, y)
    halves = (line[: side * rows // 2], line[side * rows // 2 :])
    query_states, passage_states, *halves = lax.optimization_barrier(
        (query_states, passage_states, *halves)
    )
    states = from_all(jnp.concatenate([query_states, passage_states], axis=0), "mp")
    blocks, places = ([], []), ([], [])
    held = halves

    def placed(stream):
        return place(jnp.stack(places[stream]).astype(jnp.int32), blocks[stream])

    for step in range(BLOCKS):
        behind, ahead = [
            lax.ppermute(held[stream], "dp", matchings[(step + 1 - stream) % 2])
            for stream in range(2)
        ]
        ahead, _ = lax.optimization_barrier((ahead, held[0]))
        for stream in (1, 0):
            if stream == 0 and step < BLOCKS - 1:
                behind, _ = lax.optimization_barrier((behind, ahead))
            elif stream == 0:
                weight_ahead = placed(1)
                behind, weight_ahead, states = lax.optimization_barrier(
                    (behind, weight_ahead, states)
                )
            came = (behind, ahead)[stream]
            at, is_upper = (position + 1 - stream) // 2, (position + 1 - stream) % 2
            if step == 0:
                half = halves[stream]
                came = jnp.concatenate(
                    [jnp.where(is_upper, came, half), jnp.where(is_upper, half, came)], axis=0
                )
            move = (0, 2 * is_upper - 1, 1 - 2 * is_upper, 2)[step]
            places[stream].append((at + move) % BLOCKS)
            blocks[stream].append(came)
        held = [blocks[0][-1], blocks[1][-1]]
    weights = [placed(0), weight_ahead]
    weights += [lax.ppermute(weight, "dp", other_core) for weight in weights]

    block = negatives.reshape(-1)
    order = jnp.arange(pairs, dtype=jnp.int32)
    earlier = (block[:, None] == block[None, :]) & (order[None, :] < order[:, None])
    slot = block * CAPACITY + jnp.sum(earlier.astype(jnp.int32), axis=1)
    slots = shards * CAPACITY
    in_slot = jnp.arange(slots, dtype=jnp.int32)[:, None] == slot[None, :]
    to_slot = in_slot.astype(BF16)
    positive_mask = (positives[:, None] == order[None, :]).astype(F32)

    def in_order(own, other):
        return jnp.where(core == 0, own, other), jnp.where(core == 0, other, own)

    projected, squares = zip(*[project(states, weight) for weight in weights])
    squares = sum(squares)
    own, other = jnp.concatenate(projected[:2], axis=1), jnp.concatenate(projected[2:], axis=1)
    projected = jnp.concatenate(in_order(own, other), axis=1)
    squares = sum_all(squares.reshape(-1, math.gcd(128, 2 * pairs)), "mp").reshape(-1)
    inverse = lax.rsqrt(squares[:, None] + EPSILON)
    embedded = (projected * inverse).astype(BF16)
    query, passage = embedded[:pairs], embedded[pairs:]
    part = query.shape[1]

    def exchange(message):
        columns_each = message.shape[1]
        message = message.reshape(shards, CAPACITY, columns_each)
        return swap(message, "dp").reshape(slots, columns_each)

    outgoing, query = lax.optimization_barrier((dot(to_slot, query).astype(BF16), query))
    arrived = exchange(outgoing)

    scores = jnp.concatenate([arrived, query], axis=0)
    scores = sum_all(dot(scores, passage, LAST_BOTH), "mp")
    exps = jnp.exp(SCORE_SCALE * scores)
    hard_scores, local_scores = scores[:slots], scores[slots:]
    hard_exp, local_exp = exps[:slots], exps[slots:]
    sums = jnp.sum(exps, axis=1)
    hard_totals, local_totals = sums[:slots], sums[slots:]

    scale = GRADIENT_SCALE / hard_totals
    rounded_exp = hard_exp.astype(BF16)
    hard_radial = jnp.sum(rounded_exp.astype(F32) * hard_scores, axis=1) * scale
    hard_sums = (scale[:, None] * dot(rounded_exp, passage)).astype(BF16)
    totals_out = jnp.sum(jnp.where(in_slot, local_totals[None, :], 0.0), axis=1)
    back = columns(parts_of(hard_totals, 3) + parts_of(hard_radial, 3) + parts_of(totals_out, 3))
    back = exchange(jnp.concatenate([hard_sums, back], axis=1))
    slot_totals = jnp.sum(back[:, part + 6 : part + 9].astype(F32), axis=1) + hard_totals
    back = dot(to_slot, back, FIRST_BOTH)
    hard_coef = ((GRADIENT_SCALE * hard_exp) / slot_totals[:, None]).astype(BF16)

    query_hard_totals = jnp.sum(back[:, part : part + 3], axis=1)
    totals = local_totals + query_hard_totals
    share = (query_hard_totals / totals)[:, None]
    local_coef = (
        GRADIENT_SCALE * (local_exp / totals[:, None] - positive_mask)
    ).astype(BF16)
    weighted_scores = local_coef.astype(F32) * local_scores

    query_grad = dot(local_coef, passage) + share * back[:, :part]
    query_radial = jnp.sum(weighted_scores, axis=1) + share[:, 0] * jnp.sum(
        back[:, part + 3 : part + 6], axis=1
    )
    passage_grad = dot(local_coef, query, FIRST_BOTH) + dot(hard_coef, arrived, FIRST_BOTH)
    passage_radial = jnp.sum(weighted_scores, axis=0) + jnp.sum(
        hard_coef.astype(F32) * hard_scores, axis=0
    )
    grad = jnp.concatenate([query_grad, passage_grad], axis=0)
    radial = jnp.concatenate([query_radial, passage_radial], axis=0)[:, None]
    proj_grad = (inverse * grad - projected * (inverse * inverse * radial)).astype(BF16)
    half = part // 2
    grad_own, grad_other = in_order(proj_grad[:, :half], proj_grad[:, half:])
    partial = spread(grad_own, grad_other, weights, parts)
    state_grad = jnp.sum(swap(partial, "mp").astype(F32), axis=0)
    return (state_grad[:pairs], state_grad[pairs:])


def solution(mesh):
    in_specs = (P("dp", "mp"), P("dp", "mp"), P("dp", "mp"), P("dp"), P("dp", None))
    out_specs = (P("dp", "mp"), P("dp", "mp"))
    return jax.shard_map(
        on_device, mesh=mesh, in_specs=in_specs, out_specs=out_specs, check_vma=False
    )
```

```python
import math

import jax
import jax.numpy as jnp
from jax import lax
from jax.experimental import pallas as pl
from jax.experimental.pallas import tpu as pltpu
from jax.sharding import PartitionSpec as P

CAPACITY = 2
CORES = 2
EXTRA = 128
BLOCKS = 4
SCORE_SCALE = 80.0
GRADIENT_SCALE = 2560.0
EPSILON = 1e-06
LAST_BOTH = (((1,), (1,)), ((), ()))
FIRST_BOTH = (((0,), (0,)), ((), ()))
F32 = jnp.float32
BF16 = jnp.bfloat16


def dot(a, b, dims=(((1,), (0,)), ((), ()))):
    return lax.dot_general(a, b, dims, preferred_element_type=F32)


def swap(x, axis, groups=None):
    return lax.all_to_all(
        x, axis, split_axis=0, concat_axis=0, tiled=True, axis_index_groups=groups
    )


def from_all(x, axis):
    return swap(jnp.broadcast_to(x[None], (lax.axis_size(axis),) + x.shape), axis)


def sum_all(x, axis):
    return jnp.sum(from_all(x, axis), axis=0)


def parts_of(x, count):
    out = []
    for _ in range(count):
        part = lax.reduce_precision(x, 8, 7)
        out.append(part.astype(BF16))
        x = x - part
    return out


def columns(parts):
    stacked = jnp.stack(parts, axis=1)
    return jnp.pad(stacked, ((0, 0), (0, EXTRA - len(parts))))


def lines(shards, parts):
    side = math.isqrt(shards // CORES)

    def shard(z, y, core):
        return (z * side + y) * CORES + core

    first = [
        [shard(z, y, 0) * parts + m for m in range(parts) for y in range(side)]
        for z in range(side)
    ] + [
        [shard(z, y, 1) * parts + m for m in range(parts) for z in range(side)]
        for y in range(side)
    ]

    def swaps(odd):
        partner = [((p + odd) ^ 1) - odd for p in range(side)]
        partner = [p % side for p in partner]
        out = []
        for z in range(side):
            for y in range(side):
                out.append((shard(z, y, 0), shard(partner[z], y, 0)))
                out.append((shard(z, y, 1), shard(z, partner[y], 1)))
        return out

    other_core = [(d, d ^ 1) for d in range(shards)]
    return side, first, (swaps(0), swaps(1)), other_core


def place_kernel(places, *refs):
    blocks, (weight, sems) = refs[:-2], refs[-2:]
    rows = blocks[0].shape[0]
    copies = []
    for i, block in enumerate(blocks):
        at = pl.multiple_of(places[i] * rows, rows)
        copies.append(pltpu.make_async_copy(block, weight.at[pl.ds(at, rows)], sems.at[i]))
        copies[-1].start()
    for copy in copies:
        copy.wait()


def place(places, blocks):
    rows, depth = blocks[0].shape
    anywhere = pl.BlockSpec(memory_space=pl.ANY)
    return pl.pallas_call(
        place_kernel,
        out_shape=jax.ShapeDtypeStruct((len(blocks) * rows, depth), BF16),
        in_specs=[pl.BlockSpec(memory_space=pltpu.SMEM)] + [anywhere] * len(blocks),
        out_specs=pl.BlockSpec(memory_space=pltpu.VMEM),
        scratch_shapes=[pltpu.SemaphoreType.DMA((len(blocks),))],
        compiler_params=pltpu.CompilerParams(vmem_limit_bytes=16 * 2**20),
    )(places, *blocks)


def project_kernel(states, weight, projected, squares):
    value = dot(states[0], weight[:, : states.shape[2]], LAST_BOTH)
    for part in range(1, states.shape[0]):
        at = pl.ds(part * states.shape[2], states.shape[2])
        value = value + dot(states[part], weight[:, at], LAST_BOTH)
    projected[...] = value
    total = jnp.sum(value * value, axis=1, keepdims=True)

    @pl.when(pl.program_id(0) == 0)
    def _():
        squares[...] = total

    @pl.when(pl.program_id(0) > 0)
    def _():
        squares[...] += total


def project(states, weight):
    parts, rows, _ = states.shape
    width, depth = weight.shape
    tile = min(256, width)
    return pl.pallas_call(
        project_kernel,
        grid=(width // tile,),
        out_shape=(
            jax.ShapeDtypeStruct((rows, width), F32),
            jax.ShapeDtypeStruct((rows, 1), F32),
        ),
        in_specs=[
            pl.BlockSpec(states.shape, lambda n: (0, 0, 0)),
            pl.BlockSpec((tile, depth), lambda n: (n, 0)),
        ],
        out_specs=(
            pl.BlockSpec((rows, tile), lambda n: (0, n)),
            pl.BlockSpec((rows, 1), lambda n: (0, 0)),
        ),
        compiler_params=pltpu.CompilerParams(vmem_limit_bytes=24 * 2**20),
        cost_estimate=pl.CostEstimate(
            flops=2 * rows * depth * width,
            bytes_accessed=2 * width * depth,
            transcendentals=0,
        ),
    )(states, weight)


def spread_kernel(grad_own, grad_other, *refs):
    weights, out = refs[:-1], refs[-1]
    depth = weights[0].shape[0]
    value = jnp.zeros(out.shape[1:], F32)
    for i, weight in enumerate(weights):
        grad = (grad_own, grad_other)[i // 2]
        at = pl.ds(i % 2 * depth, depth)
        value = value + dot(grad[:, at], weight[...])
    out[0] = value.astype(BF16)


def spread(grad_own, grad_other, weights, parts):
    rows, width = grad_own.shape
    depth, columns_all = weights[0].shape
    columns_each = columns_all // parts
    tile = min(1024, columns_each)
    per_part = columns_each // tile
    return pl.pallas_call(
        spread_kernel,
        grid=(parts * per_part,),
        out_shape=jax.ShapeDtypeStruct((parts, rows, columns_each), BF16),
        in_specs=[pl.BlockSpec((rows, width), lambda n: (0, 0))] * 2
        + [pl.BlockSpec((depth, tile), lambda n: (0, n))] * len(weights),
        out_specs=pl.BlockSpec((1, rows, tile), lambda n: (n // per_part, 0, n % per_part)),
        compiler_params=pltpu.CompilerParams(vmem_limit_bytes=46 * 2**20),
        cost_estimate=pl.CostEstimate(
            flops=4 * rows * width * columns_all,
            bytes_accessed=4 * width * columns_all,
            transcendentals=0,
        ),
    )(grad_own, grad_other, *weights)


def on_device(query_states, passage_states, head_weight, positives, negatives):
    pairs, width = query_states.shape
    parts = lax.axis_size("mp")
    shards = lax.axis_size("dp")
    side, first, matchings, other_core = lines(shards, parts)
    rows = head_weight.shape[0] // parts
    shard = lax.axis_index("dp")
    core = shard % CORES
    z, y = shard // (CORES * side), (shard // CORES) % side

    line = jnp.broadcast_to(
        head_weight.reshape(parts, 1, rows, width), (parts, side, rows, width)
    ).reshape(parts * side, rows, width)
    line = swap(line, ("dp", "mp"), first).reshape(parts, side, rows, width)
    line = line.transpose(1, 2, 0, 3).reshape(side * rows, parts * width)

    position = jnp.where(core == 0, z, y)
    halves = (line[: side * rows // 2], line[side * rows // 2 :])
    query_states, passage_states, *halves = lax.optimization_barrier(
        (query_states, passage_states, *halves)
    )
    states = from_all(jnp.concatenate([query_states, passage_states], axis=0), "mp")
    blocks, places = ([], []), ([], [])
    held = halves

    def placed(stream):
        return place(jnp.stack(places[stream]).astype(jnp.int32), blocks[stream])

    for step in range(BLOCKS):
        behind, ahead = [
            lax.ppermute(held[stream], "dp", matchings[(step + 1 - stream) % 2])
            for stream in range(2)
        ]
        ahead, _ = lax.optimization_barrier((ahead, held[0]))
        for stream in (1, 0):
            if stream == 0 and step < BLOCKS - 1:
                behind, _ = lax.optimization_barrier((behind, ahead))
            elif stream == 0:
                weight_ahead = placed(1)
                behind, weight_ahead, states = lax.optimization_barrier(
                    (behind, weight_ahead, states)
                )
            came = (behind, ahead)[stream]
            at, is_upper = (position + 1 - stream) // 2, (position + 1 - stream) % 2
            if step == 0:
                half = halves[stream]
                came = jnp.concatenate(
                    [jnp.where(is_upper, came, half), jnp.where(is_upper, half, came)], axis=0
                )
            move = (0, 2 * is_upper - 1, 1 - 2 * is_upper, 2)[step]
            places[stream].append((at + move) % BLOCKS)
            blocks[stream].append(came)
        held = [blocks[0][-1], blocks[1][-1]]
    weights = [placed(0), weight_ahead]
    weights += [lax.ppermute(weight, "dp", other_core) for weight in weights]

    block = negatives.reshape(-1)
    order = jnp.arange(pairs, dtype=jnp.int32)
    earlier = (block[:, None] == block[None, :]) & (order[None, :] < order[:, None])
    slot = block * CAPACITY + jnp.sum(earlier.astype(jnp.int32), axis=1)
    slots = shards * CAPACITY
    in_slot = jnp.arange(slots, dtype=jnp.int32)[:, None] == slot[None, :]
    to_slot = in_slot.astype(BF16)
    positive_mask = (positives[:, None] == order[None, :]).astype(F32)

    def in_order(own, other):
        return jnp.where(core == 0, own, other), jnp.where(core == 0, other, own)

    projected, squares = zip(*[project(states, weight) for weight in weights])
    squares = sum(squares)
    own, other = jnp.concatenate(projected[:2], axis=1), jnp.concatenate(projected[2:], axis=1)
    projected = jnp.concatenate(in_order(own, other), axis=1)
    squares = sum_all(squares.reshape(-1, math.gcd(128, 2 * pairs)), "mp").reshape(-1)
    inverse = lax.rsqrt(squares[:, None] + EPSILON)
    embedded = (projected * inverse).astype(BF16)
    query, passage = embedded[:pairs], embedded[pairs:]
    part = query.shape[1]

    def exchange(message):
        columns_each = message.shape[1]
        message = message.reshape(shards, CAPACITY, columns_each)
        return swap(message, "dp").reshape(slots, columns_each)

    outgoing, query = lax.optimization_barrier((dot(to_slot, query).astype(BF16), query))
    arrived = exchange(outgoing)

    scores = jnp.concatenate([arrived, query], axis=0)
    scores = sum_all(dot(scores, passage, LAST_BOTH), "mp")
    exps = jnp.exp(SCORE_SCALE * scores)
    hard_scores, local_scores = scores[:slots], scores[slots:]
    hard_exp, local_exp = exps[:slots], exps[slots:]
    sums = jnp.sum(exps, axis=1)
    hard_totals, local_totals = sums[:slots], sums[slots:]

    scale = GRADIENT_SCALE / hard_totals
    rounded_exp = hard_exp.astype(BF16)
    hard_radial = jnp.sum(rounded_exp.astype(F32) * hard_scores, axis=1) * scale
    hard_sums = (scale[:, None] * dot(rounded_exp, passage)).astype(BF16)
    totals_out = jnp.sum(jnp.where(in_slot, local_totals[None, :], 0.0), axis=1)
    back = columns(parts_of(hard_totals, 3) + parts_of(hard_radial, 3) + parts_of(totals_out, 3))
    back = exchange(jnp.concatenate([hard_sums, back], axis=1))
    slot_totals = jnp.sum(back[:, part + 6 : part + 9].astype(F32), axis=1) + hard_totals
    back = dot(to_slot, back, FIRST_BOTH)
    hard_coef = ((GRADIENT_SCALE * hard_exp) / slot_totals[:, None]).astype(BF16)

    query_hard_totals = jnp.sum(back[:, part : part + 3], axis=1)
    totals = local_totals + query_hard_totals
    share = (query_hard_totals / totals)[:, None]
    local_coef = (
        GRADIENT_SCALE * (local_exp / totals[:, None] - positive_mask)
    ).astype(BF16)
    weighted_scores = local_coef.astype(F32) * local_scores

    query_grad = dot(local_coef, passage) + share * back[:, :part]
    query_radial = jnp.sum(weighted_scores, axis=1) + share[:, 0] * jnp.sum(
        back[:, part + 3 : part + 6], axis=1
    )
    passage_grad = dot(local_coef, query, FIRST_BOTH) + dot(hard_coef, arrived, FIRST_BOTH)
    passage_radial = jnp.sum(weighted_scores, axis=0) + jnp.sum(
        hard_coef.astype(F32) * hard_scores, axis=0
    )
    grad = jnp.concatenate([query_grad, passage_grad], axis=0)
    radial = jnp.concatenate([query_radial, passage_radial], axis=0)[:, None]
    proj_grad = (inverse * grad - projected * (inverse * inverse * radial)).astype(BF16)
    half = part // 2
    grad_own, grad_other = in_order(proj_grad[:, :half], proj_grad[:, half:])
    partial = spread(grad_own, grad_other, weights, parts)
    state_grad = jnp.sum(swap(partial, "mp").astype(F32), axis=0)
    return (state_grad[:pairs], state_grad[pairs:])


def solution(mesh):
    in_specs = (P("dp", "mp"), P("dp", "mp"), P("dp", "mp"), P("dp"), P("dp", None))
    out_specs = (P("dp", "mp"), P("dp", "mp"))
    return jax.shard_map(
        on_device, mesh=mesh, in_specs=in_specs, out_specs=out_specs, check_vma=False
    )
```
